128 devices in a mesh: ctx: 32 (over y, z, core), tp: 4 (over x).
Axes of the slice: x: 4, y: 4, z: 4, core: 2. Of those that a mesh axis runs over, the one named last changes fastest.
Arguments:
- ctx_q: bfloat16 [24576, 8192], P('ctx', 'tp'), may hold values from -150 to 150
- ctx_k: bfloat16 [24576, 1024], P('ctx', 'tp'), may hold values from -8 to 8
- ctx_v: bfloat16 [24576, 1024], P('ctx', 'tp'), may hold values from -6 to 6
- query_q: bfloat16 [256, 8192], P('ctx', 'tp'), may hold values from -150 to 150
- query_k: bfloat16 [256, 1024], P('ctx', 'tp'), may hold values from -8 to 8
- query_v: bfloat16 [256, 1024], P('ctx', 'tp'), may hold values from -6 to 6
- out_weight: bfloat16 [8192, 8192], P('tp', 'ctx'), may hold values from -0.0625 to 0.0625
Outputs:
- ctx_out: bfloat16 [24576, 8192], P('ctx', 'tp')
- query_out: bfloat16 [256, 8192], P('tp', 'ctx')
The draws below stay inside these ranges and needn't reach their ends.
All inputs are finite; a program needn't handle non-finite values.
Results may differ from the reference program's by a relative error of at most 0.011.
Values may be sent and summed in bfloat16 or wider, within the bound.
A program may use at most 320 MiB of HBM per device.

```python
import jax
import jax.numpy as jnp
from jax import lax

D = 8192
HEADS = 64
KV_HEADS = 8
HEAD_DIM = 128
BLK = 768
QROWS = 256
CONTEXT = 24576
N_CTX = 32


def context_base(key):
    return jax.random.normal(jax.random.fold_in(key, 101), (CONTEXT, KV_HEADS * HEAD_DIM), jnp.float32)


def query_base(key):
    return jax.random.normal(jax.random.fold_in(key, 102), (QROWS, KV_HEADS * HEAD_DIM), jnp.float32)


def draw_ctx_k(key, part):
    base = context_base(key)
    return base.astype(jnp.bfloat16)


def draw_ctx_q(key, part):
    key = jax.random.fold_in(key, 4)
    return (2.5 * jax.random.normal(key, (CONTEXT, HEADS * HEAD_DIM), jnp.float32)).astype(jnp.bfloat16)


def draw_query_k(key, part):
    base = query_base(key)
    return base.astype(jnp.bfloat16)


def draw_query_q(key, part):
    key = jax.random.fold_in(key, 6)
    return (2.5 * jax.random.normal(key, (QROWS, HEADS * HEAD_DIM), jnp.float32)).astype(jnp.bfloat16)


def block_levels(stream_key, dims, split, least, top_value):
    level, own = 1.0, jax.random.fold_in(stream_key, 6)
    for position, shards_of in split:
        draws = jnp.exp(jax.random.uniform(jax.random.fold_in(own, position), (shards_of,), jnp.float32, least / len(split), top_value / len(split)))
        level = level * jnp.repeat(draws, dims[position] // shards_of).reshape([-1 if axis == position else 1 for axis in range(len(dims))])
    return level


def normal_values(own_key, dims, width, most, shards=(), kind=jnp.bfloat16):
    values = width * jax.random.normal(own_key, dims, jnp.float32)
    if shards:
        values = values * block_levels(own_key, dims, shards, -0.22, 0.18)
    return jnp.clip(values, -most, most).astype(kind)


def setup_inputs(seed: int = 0) -> dict:
    key_of = jax.random.split(jax.random.key(seed), 8)
    return {
        "ctx_q": draw_ctx_q(jax.random.fold_in(key_of[7], 71), 0),
        "ctx_k": draw_ctx_k(jax.random.fold_in(key_of[7], 71), 0),
        "ctx_v": normal_values(key_of[2], (CONTEXT, KV_HEADS * HEAD_DIM), 1.0, 6.0, ((0, 32), (1, 4))),
        "query_q": draw_query_q(jax.random.fold_in(key_of[7], 71), 0),
        "query_k": draw_query_k(jax.random.fold_in(key_of[7], 71), 0),
        "query_v": normal_values(key_of[5], (QROWS, KV_HEADS * HEAD_DIM), 1.0, 6.0, ((0, 32), (1, 4))),
        "out_weight": normal_values(key_of[6], (HEADS * HEAD_DIM, D), (HEADS * HEAD_DIM) ** -0.5, 0.0625, ((0, 4), (1, 32))),
    }


def head_stats(queries, keys, values, mask):
    scores = jnp.einsum("rgd,kd->rgk", queries.astype(jnp.float32), keys.astype(jnp.float32)) * (HEAD_DIM ** -0.5)
    if mask is not None:
        scores = jnp.where(mask[:, None, :], scores, -1e30)
    top = jnp.max(scores, axis=2)
    weights = jnp.exp(scores - top[..., None])
    total = jnp.sum(weights, axis=2)
    rounded = lax.optimization_barrier(weights.astype(jnp.bfloat16)).astype(jnp.float32)
    mixed = jnp.einsum("rgk,kd->rgd", rounded, values.astype(jnp.float32))
    return top, total, mixed


def all_heads(queries, keys, values, mask):
    group = HEADS // KV_HEADS
    rows = queries.shape[0]
    qh = queries.reshape(rows, KV_HEADS, group, HEAD_DIM)
    kh = keys.reshape(keys.shape[0], KV_HEADS, HEAD_DIM)
    vh = values.reshape(values.shape[0], KV_HEADS, HEAD_DIM)
    tops, totals, mixes = [], [], []
    for head in range(KV_HEADS):
        top, total, mixed = head_stats(qh[:, head], kh[:, head], vh[:, head], mask)
        tops.append(top)
        totals.append(total)
        mixes.append(mixed)
    return jnp.concatenate(tops, 1), jnp.concatenate(totals, 1), jnp.concatenate(mixes, 1)


def reference(ctx_q, ctx_k, ctx_v, query_q, query_k, query_v, out_weight):
    blocks = jnp.arange(N_CTX, dtype=jnp.int32)
    anchor_k = ctx_k[:BLK]
    anchor_v = ctx_v[:BLK]
    row_ids = jnp.arange(BLK, dtype=jnp.int32)[:, None]
    col_ids = jnp.arange(2 * BLK, dtype=jnp.int32)[None, :]

    def encode(block):
        start = (block * BLK).astype(jnp.int32)
        queries = lax.dynamic_slice_in_dim(ctx_q, start, BLK, 0)
        keys = jnp.concatenate([anchor_k, lax.dynamic_slice_in_dim(ctx_k, start, BLK, 0)], 0)
        values = jnp.concatenate([anchor_v, lax.dynamic_slice_in_dim(ctx_v, start, BLK, 0)], 0)
        mask = jnp.where(col_ids < BLK, block > 0, col_ids - BLK <= row_ids)
        top, total, mixed = all_heads(queries, keys, values, mask)
        return (mixed / total[..., None]).astype(jnp.bfloat16).reshape(BLK, HEADS * HEAD_DIM)

    ctx_out = lax.map(encode, blocks).reshape(N_CTX * BLK, HEADS * HEAD_DIM)

    def block_stats(block):
        start = (block * BLK).astype(jnp.int32)
        keys = lax.dynamic_slice_in_dim(ctx_k, start, BLK, 0)
        values = lax.dynamic_slice_in_dim(ctx_v, start, BLK, 0)
        return all_heads(query_q, keys, values, None)

    tops, totals, mixes = lax.map(block_stats, blocks)
    query_rows = jnp.arange(QROWS, dtype=jnp.int32)
    self_mask = query_rows[None, :] <= query_rows[:, None]
    self_top, self_total, self_mixed = all_heads(query_q, query_k, query_v, self_mask)
    peak = jnp.maximum(jnp.max(tops, axis=0), self_top)
    factors = jnp.exp(tops - peak[None])
    self_factor = jnp.exp(self_top - peak)
    numer = jnp.sum(factors[..., None] * mixes, axis=0) + self_factor[..., None] * self_mixed
    denom = jnp.sum(factors * totals, axis=0) + self_factor * self_total
    attn = (numer / denom[..., None]).astype(jnp.bfloat16).reshape(QROWS, HEADS * HEAD_DIM)
    query_out = jnp.dot(attn, out_weight, preferred_element_type=jnp.float32).astype(jnp.bfloat16)
    return ctx_out, query_out
```

```python
import functools
import math

import jax
import jax.numpy as jnp
from jax import lax
from jax.experimental import pallas as pl
from jax.experimental.pallas import tpu as pltpu
from jax.sharding import PartitionSpec as P

HD = 128
SCALE = HD**-0.5 * math.log2(math.e)
F32 = jnp.float32
BF16 = jnp.bfloat16
MESH = pl.DeviceIdType.MESH
CHUNK = 16


def dot(a, b):
    return jnp.dot(a, b, preferred_element_type=F32)


def dot_t(a, b):
    return lax.dot_general(a, b, (((1,), (1,)), ((), ())), preferred_element_type=F32)


def iota(shape, dim):
    return lax.broadcasted_iota(jnp.int32, shape, dim)


def loop(count, step):
    def body(i, carry):
        step(i)
        return carry

    lax.fori_loop(0, count, body, 0)


def kernel(
    nch, ntp, blk,
    ctx_q, ctx_k, ctx_v, query_q, query_k, query_v, weight,
    ctx_out, query_out,
    q_v, k_v, v_v, w_v, pk_v, pv_v, pw_v, out_v,
    vv_own, vv_pair, vv_anchor,
    gq, kvp, an, rs_s, rs_r, lam_v, ag, tp_s, tp_r,
    st_o, st_m,
    sa0, sa1, sa2, pa0, pa1, pa2, sb0, sb1, pb0, pb1, sq0, sq1, pq0, pq1, mq0, mq1,
    loc, pair_s, pair_r, gq_s, gq_r, an_s, an_r, sc_s, pc_r, rs_ss, rs_rs, ag_s, ag_r, tp_ss, tp_rs,
):
    me = lax.axis_index("ctx")
    tp = lax.axis_index("tp")
    chip = me // 2
    core = me % 2
    partner = me + 1 - 2 * core
    tq = blk // 3
    piece = blk // nch

    def local(i, src, dst):
        return pltpu.make_async_copy(src, dst, loc.at[i])

    half = q_v.shape[1] // 2
    lk = local(0, ctx_k, an_view(k_v, nch, piece))
    lv = local(1, ctx_v, an_view(v_v, nch, piece))
    lq0 = local(2, ctx_q.at[:, 0:half], q_v.at[:, 0:half])
    lq1 = local(3, ctx_q.at[:, half:], q_v.at[:, half:])
    lw = local(4, weight, w_v)
    for c in (lk, lv, lq0, lq1, lw):
        c.start()

    barrier = pltpu.get_barrier_semaphore()

    def greet(**where):
        pl.semaphore_signal(barrier, inc=1, device_id=where, device_id_type=MESH)

    loop(nch - 1, lambda i: greet(ctx=2 * ((chip + 1 + i) % nch) + core))
    greet(ctx=partner)

    def greet_tp(i):
        greet(tp=(tp + 1 + i) % ntp)
        greet(tp=(tp + 1 + i) % ntp, ctx=partner)

    loop(ntp - 1, greet_tp)

    @pl.when(me == 0)
    def _():
        loop(nch - 1, lambda i: greet(ctx=2 * (1 + i) + 1))

    @pl.when((core == 1) & (chip > 0))
    def _():
        greet(ctx=0)

    x = query_q[...].astype(F32)
    gq[chip, 0:HD, :] = jnp.concatenate([x[:, h * HD : (h + 1) * HD] for h in range(16)], 0).astype(BF16)
    xk = query_k[...].astype(F32)
    xv = query_v[...].astype(F32)
    gq[chip, HD : HD + 32, :] = jnp.concatenate([xk[:, :HD], xk[:, HD:], xv[:, :HD], xv[:, HD:]], 0).astype(BF16)

    extra = jnp.where(me == 0, nch - 1, jnp.where((core == 1) & (chip > 0), 1, 0))
    pl.semaphore_wait(barrier, nch - 1 + 1 + 2 * (ntp - 1) + extra)

    def remote(src, dst, send, recv, **where):
        return pltpu.make_async_remote_copy(
            src_ref=src, dst_ref=dst, send_sem=send, recv_sem=recv, device_id=where, device_id_type=MESH
        )

    def peer_copy(i, src, dst, send, recv):
        return remote(src, dst, send.at[i], recv.at[chip], ctx=2 * ((chip + 1 + i) % nch) + core)

    def start_peers(src, dst, send, recv):
        loop(nch - 1, lambda i: peer_copy(i, src, dst, send, recv).start())

    def sent_peers(src, dst, send, recv):
        loop(nch - 1, lambda i: peer_copy(i, src, dst, send, recv).wait_send())

    def recv_peers(buf, send, recv):
        def step(i):
            j = (chip + 1 + i) % nch
            remote(buf(j), buf(j), send.at[i], recv.at[j], ctx=2 * j + core).wait_recv()

        loop(nch - 1, step)

    def pair_copy(i, src, dst):
        return remote(src, dst, pair_s.at[i], pair_r.at[i], ctx=partner)

    own_piece = an.at[core, chip]

    def scatter_copies(j):
        ck = remote(ctx_k.at[j], an.at[0, j], sc_s.at[0, j], pc_r.at[0], ctx=2 * j)
        cv = remote(ctx_v.at[j], an.at[1, j], sc_s.at[1, j], pc_r.at[0], ctx=2 * j + 1)
        return ck, cv

    first_key = pltpu.make_async_copy(ctx_k.at[0], an.at[0, 0], pc_r.at[0])

    @pl.when(me == 0)
    def _():
        first_key.start()
        scatter_copies(0)[1].start()

        def step(i):
            ck, cv = scatter_copies(1 + i)
            ck.start()
            cv.start()

        loop(nch - 1, step)

    mine = gq.at[chip]
    start_peers(mine, mine, gq_s, gq_r)
    pk_c = pair_copy(0, ctx_k, an_view(pk_v, nch, piece))
    pv_c = pair_copy(1, ctx_v, an_view(pv_v, nch, piece))
    pk_c.start()
    pv_c.start()

    def fill(vv, v):
        for g in range(2):
            vv[g, :, 0:HD] = v[:, g * HD : (g + 1) * HD]
            vv[g, :, HD:] = jnp.ones((blk, HD), BF16)

    s_a, p_a = (sa0, sa1, sa2), (pa0, pa1, pa2)

    def head_cols(g):
        return pl.ds(pl.multiple_of(g * HD, HD), HD)

    def a_scores(hp, i):
        n = tq * (i + 1)
        q = q_v[i * tq : n, pl.ds(pl.multiple_of(hp * 2 * HD, 2 * HD), 2 * HD)]
        q = jnp.concatenate([q[:, :HD], q[:, HD:]], 0)
        s_a[i][...] = dot_t(q, k_v[0:n, head_cols(hp // 4)])

    def a_soft(hp, i):
        n = tq * (i + 1)
        for r in range(2 * tq // CHUNK):
            low = r * CHUNK
            s = s_a[i][low : low + CHUNK, :]
            keep = iota((CHUNK, tq), 1) <= iota((CHUNK, tq), 0) + low % tq
            d = jnp.where(keep, s[:, n - tq :], -1e30)
            s = d if i == 0 else jnp.concatenate([s[:, : n - tq], d], 1)
            m = jnp.max(s, axis=1, keepdims=True)
            p_a[i][low : low + CHUNK, :] = jnp.exp2((s - m) * SCALE).astype(BF16)
            at = i * tq + low % tq
            st_m[2 * hp + low // tq, at : at + CHUNK, :] = jnp.broadcast_to(m, (CHUNK, HD))

    def a_mix(hp, i):
        n = tq * (i + 1)
        o = dot(p_a[i][...], vv_own[hp // 4, 0:n, :])
        st_o[2 * hp, i * tq : n, :] = o[:tq]
        st_o[2 * hp + 1, i * tq : n, :] = o[tq:]

    def own_block(first, last):
        a_scores(first, 0)

        def step(j):
            hp = first + j
            a_scores(hp, 1)
            a_soft(hp, 0)
            a_mix(hp, 0)
            a_scores(hp, 2)
            a_soft(hp, 1)
            a_mix(hp, 1)
            a_scores(jnp.minimum(hp + 1, last - 1), 0)
            a_soft(hp, 2)
            a_mix(hp, 2)

        loop(last - first, step)

    lk.wait()
    lv.wait()
    fill(vv_own, v_v)
    lq0.wait()
    own_block(0, 2)

    piece_in = remote(own_piece, own_piece, sc_s.at[0, 0], pc_r.at[0], ctx=partner)

    @pl.when(me == 0)
    def _():
        first_key.wait()

    @pl.when(me != 0)
    def _():
        piece_in.wait_recv()

    start_peers(own_piece, own_piece, an_s, an_r)
    own_block(2, 4)

    lq1.wait()
    recv_peers(lambda j: gq.at[j], gq_s, gq_r)
    pk_c.wait_recv()
    pv_c.wait_recv()
    fill(vv_pair, pv_v)
    kv_c = pair_copy(2, gq.at[:, HD : HD + 32, :], kvp)
    kv_c.start()
    w_c = pair_copy(3, weight, pw_v)
    w_c.start()

    s_q, p_q, m_q = (sq0, sq1), (pq0, pq1), (mq0, mq1)
    per_g = nch // 4

    def q_scores(it, b):
        g, t = it // per_g, it % per_g
        q = gq[pl.ds(4 * t, 4), pl.ds(pl.multiple_of(g * 64, 64), 64), :].reshape(256, HD)
        s_q[b][:, 0:blk] = dot_t(q, k_v[:, head_cols(g)])
        s_q[b][:, blk:] = dot_t(q, pk_v[:, head_cols(g)])

    def q_soft(b):
        for r in range(256 // CHUNK):
            rows = slice(r * CHUNK, (r + 1) * CHUNK)
            s = s_q[b][rows, :]
            m = jnp.max(s, axis=1, keepdims=True)
            p_q[b][rows, :] = jnp.exp2((s - m) * SCALE).astype(BF16)
            m_q[b][rows, :] = jnp.broadcast_to(m, (CHUNK, HD))

    def q_mix(it, b):
        g, t = it // per_g, it % per_g
        o = dot(p_q[b][:, 0:blk], vv_own[g]) + dot(p_q[b][:, blk:], vv_pair[g])
        total = o[:, HD:]
        lam = m_q[b][...] * SCALE + jnp.log2(total)
        o = (o[:, :HD] / total).astype(BF16)
        spot = iota((64, HD), 1) - g * 64 == iota((64, HD), 0)
        for u in range(4):
            rs_s[4 * t + u, pl.ds(pl.multiple_of(g * 64, 64), 64), :] = o[u * 64 : (u + 1) * 64]
            row = jnp.sum(jnp.where(spot, lam[u * 64 : (u + 1) * 64], 0.0), axis=0, keepdims=True)
            lam_v[4 * t + u, pl.ds(g, 1), :] = row

    q_scores(0, 0)

    def q_step(j):
        q_scores(2 * j + 1, 1)
        q_soft(0)
        q_mix(2 * j, 0)
        q_scores(jnp.minimum(2 * j + 2, 2 * per_g - 1), 0)
        q_soft(1)
        q_mix(2 * j + 1, 1)

    loop(per_g, q_step)

    def split3(lam):
        hi = lam.astype(BF16).astype(F32)
        mid = (lam - hi).astype(BF16).astype(F32)
        return hi, mid, lam - hi - mid

    hi, mid, low = split3(lam_v[:, 0:1, :] + lam_v[:, 1:2, :])
    row = iota((nch, 16, HD), 1)
    stats = jnp.where(row == 0, hi, jnp.where(row == 1, mid, jnp.where(row == 2, low, 0.0)))
    rs_s[:, HD : HD + 16, :] = stats.astype(BF16)

    def rs_copy(i):
        j = (chip + 1 + i) % nch
        return remote(rs_s.at[j], rs_r.at[chip], rs_ss.at[i], rs_rs.at[chip], ctx=2 * j + core)

    loop(nch - 1, lambda i: rs_copy(i).start())
    rs_r[pl.ds(chip, 1)] = rs_s[pl.ds(chip, 1)]

    own_block(4, 6)
    recv_peers(lambda j: an.at[core, j], an_s, an_r)
    an_c = pair_copy(4, an.at[core], an.at[core])
    an_c.start()
    own_block(6, 8)
    an_c.wait_send()
    remote(an.at[1 - core], an.at[1 - core], pair_s.at[4], pair_r.at[4], ctx=partner).wait_recv()

    for g in range(2):
        vv_anchor[g, :, 0:HD] = an[1, :, :, g * HD : (g + 1) * HD].reshape(blk, HD)
        vv_anchor[g, :, HD:] = jnp.ones((blk, HD), BF16)

    s_b, p_b = (sb0, sb1), (pb0, pb1)

    def b_scores(h, b):
        q = q_v[:, pl.ds(pl.multiple_of(h * HD, HD), HD)]
        keys = an[0, :, :, head_cols(h // 8)].reshape(blk, HD)
        s_b[b][...] = dot_t(q, keys)

    def b_soft(h, b):
        for r in range(blk // CHUNK):
            rows = slice(r * CHUNK, (r + 1) * CHUNK)
            s = s_b[b][rows, :]
            old = st_m[h, rows, :]
            m = jnp.maximum(jnp.max(s, axis=1, keepdims=True), old[:, 0:1])
            p_b[b][rows, :] = jnp.exp2((s - m) * SCALE).astype(BF16)
            st_m[h, rows, :] = jnp.exp2((old - m) * SCALE)

    def b_mix(h, b):
        o = dot(p_b[b][...], vv_anchor[h // 8])
        factor = st_m[h]
        top = factor * st_o[h, :, 0:HD] + o[:, :HD]
        total = factor * st_o[h, :, HD:] + o[:, HD:]
        out_v[:, pl.ds(pl.multiple_of(h * HD, HD), HD)] = (top / total).astype(BF16)

    def anchor_block(first, last):
        @pl.when(me != 0)
        def _():
            b_scores(first, 0)

            def step(j):
                h = first + 2 * j
                b_scores(h + 1, 1)
                b_soft(h, 0)
                b_mix(h, 0)
                b_scores(jnp.minimum(h + 2, last - 1), 0)
                b_soft(h + 1, 1)
                b_mix(h + 1, 1)

            loop((last - first) // 2, step)

        @pl.when(me == 0)
        def _():
            def step(j):
                h = first + j
                value = st_o[h, :, 0:HD] / st_o[h, :, HD:]
                out_v[:, pl.ds(pl.multiple_of(h * HD, HD), HD)] = value.astype(BF16)

            loop(last - first, step)

    anchor_block(0, 8)
    out0 = local(5, out_v.at[:, 0:half], ctx_out.at[:, 0:half])
    out0.start()

    kv_c.wait_recv()

    def self_part():
        kv_own = gq[:, HD : HD + 32, :].astype(F32)
        kv_pair = kvp[...].astype(F32)
        outs, lams = [], []
        count = 16 * nch
        f = iota((64, count), 1)
        second = f // (8 * nch)
        token = (2 * ((f // 8) % nch) + jnp.where(second == 0, core, 1 - core)) * 8 + f % 8
        keep = token <= 8 * me + iota((64, count), 0) % 8
        for g in range(2):
            def pick(first):
                a = kv_own[:, first : first + 8, :].reshape(8 * nch, HD)
                b = kv_pair[:, first : first + 8, :].reshape(8 * nch, HD)
                return jnp.concatenate([a, b], 0).astype(BF16)

            q = gq[chip, g * 64 : (g + 1) * 64, :]
            s = jnp.where(keep, dot_t(q, pick(8 * g)), -1e30)
            m = jnp.max(s, axis=1, keepdims=True)
            p = jnp.exp2((s - m) * SCALE)
            total = jnp.sum(p, axis=1, keepdims=True)
            outs.append((dot(p.astype(BF16), pick(16 + 8 * g)) / total).astype(BF16))
            lam = jnp.broadcast_to(m * SCALE + jnp.log2(total), (64, HD))
            spot = iota((64, HD), 1) - g * 64 == iota((64, HD), 0)
            lams.append(jnp.sum(jnp.where(spot, lam, 0.0), axis=0, keepdims=True))
        return jnp.concatenate(outs, 0), lams[0] + lams[1]

    self_o, self_lam = self_part()
    recv_peers(lambda j: rs_r.at[j], rs_ss, rs_rs)
    stat = rs_r[:, HD : HD + 16, :].astype(F32)
    lam = stat[:, 0, :] + stat[:, 1, :] + stat[:, 2, :]
    peak = jnp.maximum(jnp.max(lam, axis=0, keepdims=True), self_lam)
    share = jnp.exp2(lam - peak)
    self_share = jnp.exp2(self_lam - peak)
    total = jnp.sum(share, axis=0, keepdims=True) + self_share
    eye = iota((HD, HD), 0) == iota((HD, HD), 1)

    def diagonal(v):
        d = jnp.where(eye, jnp.broadcast_to(v, (HD, HD)), 0.0)
        d_hi = d.astype(BF16)
        return jnp.concatenate([d_hi, (d - d_hi.astype(F32)).astype(BF16)], 1)

    acc = dot(diagonal(self_share / total), jnp.concatenate([self_o, self_o], 0))
    share = share / total
    for j in range(nch):
        o = rs_r[j, 0:HD, :]
        acc = acc + dot(diagonal(share[j : j + 1]), jnp.concatenate([o, o], 0))
    ag[pl.ds(chip, 1)] = acc.astype(BF16)[None]
    ag_mine = ag.at[chip]
    start_peers(ag_mine, ag_mine, ag_s, ag_r)

    anchor_block(8, 12)

    recv_peers(lambda j: ag.at[j], ag_s, ag_r)
    w_c.wait_recv()
    lw.wait()
    rows = 8 * nch
    parts = [jnp.zeros((rows, w_v.shape[1]), F32)] * 2
    for hp in range(8):
        both = ag[:, 16 * hp : 16 * hp + 16, :].astype(F32)
        a = jnp.concatenate([both[:, 0:8, :].reshape(rows, HD), both[:, 8:16, :].reshape(rows, HD)], 1).astype(BF16)
        for c, w in enumerate((w_v, pw_v)):
            parts[c] = parts[c] + dot(a, w[hp * 2 * HD : (hp + 1) * 2 * HD, :])
    part = rows // ntp
    for c in range(2):
        for t in range(ntp):
            tp_s[c, t] = parts[c][t * part : (t + 1) * part]

    def tp_copy(i, c):
        t = (tp + 1 + i) % ntp if c == 0 else (tp + i) % ntp
        where = {"tp": t} if c == 0 else {"tp": t, "ctx": partner}
        return remote(tp_s.at[c, t], tp_r.at[c, tp], tp_ss.at[c, i], tp_rs.at[c, tp], **where)

    loop(ntp - 1, lambda i: tp_copy(i, 0).start())
    loop(ntp, lambda i: tp_copy(i, 1).start())

    anchor_block(12, 16)
    out1 = local(6, out_v.at[:, half:], ctx_out.at[:, half:])
    out1.start()

    def tp_recv(c, t):
        buf = tp_r.at[c, t]
        where = {"tp": t} if c == 0 else {"tp": t, "ctx": partner}
        remote(buf, buf, tp_ss.at[c, 0], tp_rs.at[c, t], **where).wait_recv()

    loop(ntp - 1, lambda i: tp_recv(0, (tp + 1 + i) % ntp))
    loop(ntp, lambda i: tp_recv(1, i))
    tp_r[0, pl.ds(tp, 1)] = tp_s[0, pl.ds(tp, 1)]
    mine_sum = jnp.sum(tp_r[0], axis=0)
    pair_sum = jnp.sum(tp_r[1], axis=0)
    groups = part // 8
    even = jnp.where(core == 0, mine_sum, pair_sum).reshape(groups, 1, 8, -1)
    odd = jnp.where(core == 0, pair_sum, mine_sum).reshape(groups, 1, 8, -1)
    query_out[...] = jnp.concatenate([even, odd], 1).reshape(2 * part, -1).astype(BF16)

    sent_peers(mine, mine, gq_s, gq_r)
    sent_peers(own_piece, own_piece, an_s, an_r)
    sent_peers(ag_mine, ag_mine, ag_s, ag_r)
    loop(nch - 1, lambda i: rs_copy(i).wait_send())
    loop(ntp - 1, lambda i: tp_copy(i, 0).wait_send())
    loop(ntp, lambda i: tp_copy(i, 1).wait_send())
    for c in (pk_c, pv_c, kv_c, w_c):
        c.wait_send()

    @pl.when(me == 0)
    def _():
        scatter_copies(0)[1].wait_send()

        def step(i):
            ck, cv = scatter_copies(1 + i)
            ck.wait_send()
            cv.wait_send()

        loop(nch - 1, step)

    out0.wait()
    out1.wait()


def an_view(ref, nch, piece):
    return ref.reshape(nch, piece, ref.shape[-1])


def body(nch, ntp, ctx_q, ctx_k, ctx_v, query_q, query_k, query_v, weight):
    blk, width = ctx_q.shape
    cols = ctx_k.shape[1]
    tq = blk // 3
    piece = blk // nch
    part = 8 * nch // ntp
    vmem = pltpu.VMEM
    dma = pltpu.SemaphoreType.DMA
    scratch = [
        vmem((blk, width), BF16), vmem((blk, cols), BF16), vmem((blk, cols), BF16), vmem(weight.shape, BF16),
        vmem((blk, cols), BF16), vmem((blk, cols), BF16), vmem(weight.shape, BF16), vmem((blk, width), BF16),
        vmem((2, blk, 2 * HD), BF16), vmem((2, blk, 2 * HD), BF16), vmem((2, blk, 2 * HD), BF16),
        vmem((nch, HD + 32, HD), BF16), vmem((nch, 32, HD), BF16), vmem((2, nch, piece, cols), BF16),
        vmem((nch, HD + 16, HD), BF16), vmem((nch, HD + 16, HD), BF16), vmem((nch, 8, HD), F32),
        vmem((nch, HD, HD), BF16), vmem((2, ntp, part, weight.shape[1]), F32), vmem((2, ntp, part, weight.shape[1]), F32),
        vmem((16, blk, 2 * HD), F32), vmem((16, blk, HD), F32),
    ]
    scratch += [vmem((2 * tq, tq * i), F32) for i in (1, 2, 3)] + [vmem((2 * tq, tq * i), BF16) for i in (1, 2, 3)]
    scratch += [vmem((blk, blk), F32)] * 2 + [vmem((blk, blk), BF16)] * 2
    scratch += [vmem((256, 2 * blk), F32)] * 2 + [vmem((256, 2 * blk), BF16)] * 2 + [vmem((256, HD), F32)] * 2
    scratch += [
        dma((7,)), dma((5,)), dma((5,)), dma((nch,)), dma((nch,)), dma((nch,)), dma((nch,)), dma((2, nch)), dma((1,)),
        dma((nch,)), dma((nch,)), dma((nch,)), dma((nch,)), dma((2, ntp)), dma((2, ntp)),
    ]
    hbm = pl.BlockSpec(memory_space=pl.ANY)
    near = pl.BlockSpec(memory_space=pltpu.VMEM)
    return pl.pallas_call(
        functools.partial(kernel, nch, ntp, blk),
        out_shape=(
            jax.ShapeDtypeStruct((blk, width), BF16),
            jax.ShapeDtypeStruct((2 * part, weight.shape[1]), BF16),
        ),
        in_specs=[hbm, hbm, hbm, near, near, near, hbm],
        out_specs=(hbm, near),
        scratch_shapes=scratch,
        compiler_params=pltpu.CompilerParams(
            collective_id=0, has_side_effects=True, vmem_limit_bytes=62 * 2**20
        ),
        name="star",
    )(
        ctx_q, ctx_k.reshape(nch, piece, cols), ctx_v.reshape(nch, piece, cols),
        query_q, query_k, query_v, weight,
    )


def solution(mesh):
    nch, ntp = mesh.shape["ctx"] // 2, mesh.shape["tp"]
    return jax.shard_map(
        functools.partial(body, nch, ntp),
        mesh=mesh,
        in_specs=(P("ctx", "tp"),) * 6 + (P("tp", "ctx"),),
        out_specs=(P("ctx", "tp"), P("tp", "ctx")),
        check_vma=False,
    )
```

```python
import functools
import math

import jax
import jax.numpy as jnp
from jax import lax
from jax.experimental import pallas as pl
from jax.experimental.pallas import tpu as pltpu
from jax.sharding import PartitionSpec as P

HD = 128
SCALE = HD**-0.5 * math.log2(math.e)
F32 = jnp.float32
BF16 = jnp.bfloat16
MESH = pl.DeviceIdType.MESH
CHUNK = 16


def dot(a, b):
    return jnp.dot(a, b, preferred_element_type=F32)


def dot_t(a, b):
    return lax.dot_general(a, b, (((1,), (1,)), ((), ())), preferred_element_type=F32)


def iota(shape, dim):
    return lax.broadcasted_iota(jnp.int32, shape, dim)


def loop(count, step):
    def body(i, carry):
        step(i)
        return carry

    lax.fori_loop(0, count, body, 0)


def kernel(
    nch, ntp, blk,
    ctx_q, ctx_k, ctx_v, query_q, query_k, query_v, weight,
    ctx_out, query_out,
    q_v, k_v, v_v, w_v, pk_v, pv_v, pw_v, out_v,
    vv_own, vv_pair, vv_anchor,
    qg, kvg, kvp, an, rs_s, rs_r, lam_v, ag, tp_s, tp_r,
    st_o, st_m,
    sa0, sa1, sa2, pa0, pa1, pa2, sb0, sb1, pb0, pb1, sq0, sq1, pq0, pq1, mq0, mq1,
    loc, pair_s, pair_r, ex_s, ex_r, sc_s, pc_r, tp_ss, tp_rs,
):
    me = lax.axis_index("ctx")
    tp = lax.axis_index("tp")
    chip = me // 2
    core = me % 2
    partner = me + 1 - 2 * core
    tq = blk // 3
    piece = blk // nch
    half = q_v.shape[1] // 2

    def local(i, src, dst):
        return pltpu.make_async_copy(src, dst, loc.at[i])

    def half_cols(g):
        return pl.ds(pl.multiple_of(g * HD, HD), HD)

    lk = local(0, ctx_k, an_view(k_v, nch, piece))
    lv = local(1, ctx_v, an_view(v_v, nch, piece))
    lq0 = local(2, ctx_q.at[:, 0:half], q_v.at[:, 0:half])
    lq1 = local(3, ctx_q.at[:, half:], q_v.at[:, half:])
    lw = local(4, weight, w_v)
    out0 = local(5, out_v.at[:, 0:half], ctx_out.at[:, 0:half])
    out1 = local(6, out_v.at[:, half:], ctx_out.at[:, half:])

    def first_key(g):
        return pltpu.make_async_copy(ctx_k.at[0, :, half_cols(g)], an.at[0, g, 0], loc.at[7 + g])

    for c in (lk, lv, lq0, lq1, lw):
        c.start()

    barrier = pltpu.get_barrier_semaphore()

    def greet(**where):
        pl.semaphore_signal(barrier, inc=1, device_id=where, device_id_type=MESH)

    loop(nch - 1, lambda i: greet(ctx=2 * ((chip + 1 + i) % nch) + core))
    greet(ctx=partner)

    def greet_tp(i):
        greet(tp=(tp + 1 + i) % ntp)
        greet(tp=(tp + 1 + i) % ntp, ctx=partner)

    loop(ntp - 1, greet_tp)

    @pl.when(me == 0)
    def _():
        loop(nch - 1, lambda i: greet(ctx=2 * (1 + i) + 1))

    @pl.when((core == 1) & (chip > 0))
    def _():
        greet(ctx=0)

    x = query_q[...].astype(F32)
    for g in range(2):
        rows = [x[:, h * HD : (h + 1) * HD] for h in range(8 * g, 8 * g + 8)]
        qg[g, chip] = jnp.concatenate(rows, 0).astype(BF16)
    xk = query_k[...].astype(F32)
    xv = query_v[...].astype(F32)
    kvg[chip] = jnp.concatenate([xk[:, :HD], xk[:, HD:], xv[:, :HD], xv[:, HD:]], 0).astype(BF16)

    def remote(src, dst, send, recv, **where):
        return pltpu.make_async_remote_copy(
            src_ref=src, dst_ref=dst, send_sem=send, recv_sem=recv, device_id=where, device_id_type=MESH
        )

    def pair_copy(i, src, dst):
        return remote(src, dst, pair_s.at[i], pair_r.at[i], ctx=partner)

    class Spread:
        def __init__(self, index, src, dst):
            self.index, self.src, self.dst = index, src, dst

        def copy(self, i):
            j = (chip + 1 + i) % nch
            send, recv = ex_s.at[self.index, i], ex_r.at[self.index, chip]
            return remote(self.src(j), self.dst(chip), send, recv, ctx=2 * j + core)

        def start(self):
            loop(nch - 1, lambda i: self.copy(i).start())

        def wait_send(self):
            loop(nch - 1, lambda i: self.copy(i).wait_send())

        def wait_recv(self):
            def step(i):
                j = (chip + 1 + i) % nch
                buf = self.dst(j)
                remote(buf, buf, ex_s.at[self.index, i], ex_r.at[self.index, j], ctx=2 * j + core).wait_recv()

            loop(nch - 1, step)

    def queries(g):
        return Spread(g, lambda j: qg.at[g, chip], lambda c: qg.at[g, c])

    def anchors(g):
        return Spread(2 + g, lambda j: an.at[core, g, chip], lambda c: an.at[core, g, c])

    def partials(g):
        return Spread(4 + g, lambda j: rs_s.at[g, j], lambda c: rs_r.at[g, c])

    def merged(g):
        return Spread(6 + g, lambda j: ag.at[g, chip], lambda c: ag.at[g, c])

    query_kv = Spread(8, lambda j: kvg.at[chip], lambda c: kvg.at[c])

    def scatter_copies(g, j):
        ck = remote(ctx_k.at[j, :, half_cols(g)], an.at[0, g, j], sc_s.at[g, 0, j], pc_r.at[g], ctx=2 * j)
        cv = remote(ctx_v.at[j, :, half_cols(g)], an.at[1, g, j], sc_s.at[g, 1, j], pc_r.at[g], ctx=2 * j + 1)
        return ck, cv

    def scatter(g):
        @pl.when(me == 0)
        def _():
            first_key(g).start()
            scatter_copies(g, 0)[1].start()

            def step(i):
                ck, cv = scatter_copies(g, 1 + i)
                ck.start()
                cv.start()

            loop(nch - 1, step)

    pk_c = pair_copy(0, ctx_k, an_view(pk_v, nch, piece))
    pv_c = pair_copy(1, ctx_v, an_view(pv_v, nch, piece))
    kv_c = pair_copy(2, kvg, kvp)
    w_c = pair_copy(3, weight, pw_v)

    def anchor_pair(g):
        return pair_copy(4 + g, an.at[core, g], an.at[core, g])

    def begin():
        extra = jnp.where(me == 0, nch - 1, jnp.where((core == 1) & (chip > 0), 1, 0))
        pl.semaphore_wait(barrier, nch - 1 + 1 + 2 * (ntp - 1) + extra)
        scatter(0)
        queries(0).start()
        pk_c.start()
        pv_c.start()
        scatter(1)
        queries(1).start()
        query_kv.start()

    def hand_on(g):
        @pl.when(me == 0)
        def _():
            first_key(g).wait()

        @pl.when(me != 0)
        def _():
            own = an.at[core, g, chip]
            remote(own, own, sc_s.at[g, 0, 0], pc_r.at[g], ctx=partner).wait_recv()

        anchors(g).start()

    def fill(vv, v):
        for g in range(2):
            vv[g, :, 0:HD] = v[:, g * HD : (g + 1) * HD]
            vv[g, :, HD:] = jnp.ones((blk, HD), BF16)

    s_a, p_a = (sa0, sa1, sa2), (pa0, pa1, pa2)

    def a_scores(hp, i):
        n = tq * (i + 1)
        q = q_v[i * tq : n, pl.ds(pl.multiple_of(hp * 2 * HD, 2 * HD), 2 * HD)]
        q = jnp.concatenate([q[:, :HD], q[:, HD:]], 0)
        s_a[i][...] = dot_t(q, k_v[0:n, half_cols(hp // 4)])

    def a_soft(hp, i):
        n = tq * (i + 1)
        for r in range(2 * tq // CHUNK):
            low = r * CHUNK
            s = s_a[i][low : low + CHUNK, :]
            keep = iota((CHUNK, tq), 1) <= iota((CHUNK, tq), 0) + low % tq
            d = jnp.where(keep, s[:, n - tq :], -1e30)
            s = d if i == 0 else jnp.concatenate([s[:, : n - tq], d], 1)
            m = jnp.max(s, axis=1, keepdims=True)
            p_a[i][low : low + CHUNK, :] = jnp.exp2((s - m) * SCALE).astype(BF16)
            at = i * tq + low % tq
            st_m[2 * hp + low // tq, at : at + CHUNK, :] = jnp.broadcast_to(m, (CHUNK, HD))

    def a_mix(hp, i):
        n = tq * (i + 1)
        o = dot(p_a[i][...], vv_own[hp // 4, 0:n, :])
        st_o[2 * hp, i * tq : n, :] = o[:tq]
        st_o[2 * hp + 1, i * tq : n, :] = o[tq:]

    s_q, p_q, m_q = (sq0, sq1), (pq0, pq1), (mq0, mq1)
    per_g = nch // 4

    def q_scores(g, t, b):
        q = qg[g, pl.ds(4 * t, 4)].reshape(256, HD)
        s_q[b][:, 0:blk] = dot_t(q, k_v[:, half_cols(g)])
        s_q[b][:, blk:] = dot_t(q, pk_v[:, half_cols(g)])

    def q_soft(b):
        for r in range(256 // CHUNK):
            rows = slice(r * CHUNK, (r + 1) * CHUNK)
            s = s_q[b][rows, :]
            m = jnp.max(s, axis=1, keepdims=True)
            p_q[b][rows, :] = jnp.exp2((s - m) * SCALE).astype(BF16)
            m_q[b][rows, :] = jnp.broadcast_to(m, (CHUNK, HD))

    twice = iota((64, HD), 1) % 64 == iota((64, HD), 0)
    first = iota((1, HD), 1) < 64

    def as_row(column):
        return jnp.sum(jnp.where(twice, column, 0.0), axis=0, keepdims=True)

    def q_mix(g, t, b):
        o = dot(p_q[b][:, 0:blk], vv_own[g]) + dot(p_q[b][:, blk:], vv_pair[g])
        total = o[:, HD:]
        lam = m_q[b][...] * SCALE + jnp.log2(total)
        o = (o[:, :HD] / total).astype(BF16)
        for u in range(4):
            rs_s[g, 4 * t + u, 0:64, :] = o[u * 64 : (u + 1) * 64]
            lam_v[4 * t + u, 0:1, :] = as_row(lam[u * 64 : (u + 1) * 64])

    def query_half(g):
        queries(g).wait_recv()

        @pl.when(g == 0)
        def _():
            pk_c.wait_recv()
            pv_c.wait_recv()
            fill(vv_pair, pv_v)

        q_scores(g, 0, 0)

        def step(j):
            q_scores(g, 2 * j + 1, 1)
            q_soft(0)
            q_mix(g, 2 * j, 0)
            q_scores(g, jnp.minimum(2 * j + 2, per_g - 1), 0)
            q_soft(1)
            q_mix(g, 2 * j + 1, 1)

        loop(per_g // 2, step)
        lam = lam_v[:, 0:1, :]
        hi = lam.astype(BF16).astype(F32)
        mid = (lam - hi).astype(BF16).astype(F32)
        row = iota((nch, 16, HD), 1)
        stats = jnp.where(row == 0, hi, jnp.where(row == 1, mid, jnp.where(row == 2, lam - hi - mid, 0.0)))
        rs_s[g, :, 64:80, :] = stats.astype(BF16)
        partials(g).start()
        rs_r[g, pl.ds(chip, 1)] = rs_s[g, pl.ds(chip, 1)]

    def anchors_across(g):
        anchors(g).wait_recv()
        anchor_pair(g).start()

    early = (114 - 7 * tp - 9 * (chip // 4) - 18 * (chip % 4)) // 28
    early = jnp.maximum(0, jnp.minimum(4, early))
    at_piece = jnp.maximum(2, early + 1)
    at_query = jnp.maximum(4, at_piece + 1)

    lk.wait()
    lv.wait()
    fill(vv_own, v_v)
    lq0.wait()
    a_scores(0, 0)

    def own_step(j):
        @pl.when(j > 0)
        def _():
            hp = j - 1
            a_scores(hp, 1)
            a_soft(hp, 0)
            a_mix(hp, 0)
            a_scores(hp, 2)
            a_soft(hp, 1)
            a_mix(hp, 1)
            a_scores(jnp.minimum(hp + 1, 7), 0)
            a_soft(hp, 2)
            a_mix(hp, 2)

        pl.when(j == 3)(lq1.wait)
        pl.when(j == early)(begin)
        pl.when(j == at_piece)(lambda: hand_on(0))
        pl.when(j == at_piece + 1)(lambda: hand_on(1))

        @pl.when(j == at_query)
        def _():
            loop(2, query_half)
            query_kv.wait_recv()
            anchors_across(0)
            anchors_across(1)
            kv_c.start()
            w_c.start()

    loop(9, own_step)

    s_b, p_b = (sb0, sb1), (pb0, pb1)

    def b_scores(h, b):
        q = q_v[:, pl.ds(pl.multiple_of(h * HD, HD), HD)]
        s_b[b][...] = dot_t(q, an[0, h // 8].reshape(blk, HD))

    def b_soft(h, b):
        for r in range(blk // CHUNK):
            rows = slice(r * CHUNK, (r + 1) * CHUNK)
            s = s_b[b][rows, :]
            old = st_m[h, rows, :]
            m = jnp.maximum(jnp.max(s, axis=1, keepdims=True), old[:, 0:1])
            p_b[b][rows, :] = jnp.exp2((s - m) * SCALE).astype(BF16)
            st_m[h, rows, :] = jnp.exp2((old - m) * SCALE)

    def b_mix(h, b):
        o = dot(p_b[b][...], vv_anchor[h // 8])
        factor = st_m[h]
        top = factor * st_o[h, :, 0:HD] + o[:, :HD]
        total = factor * st_o[h, :, HD:] + o[:, HD:]
        out_v[:, pl.ds(pl.multiple_of(h * HD, HD), HD)] = (top / total).astype(BF16)

    def anchor_in(g):
        other = an.at[1 - core, g]
        remote(other, other, pair_s.at[4 + g], pair_r.at[4 + g], ctx=partner).wait_recv()
        vv_anchor[g, :, 0:HD] = an[1, g].reshape(blk, HD)
        vv_anchor[g, :, HD:] = jnp.ones((blk, HD), BF16)

    def self_half(g):
        count = 16 * nch
        f = iota((64, count), 1)
        side = jnp.where(f // (8 * nch) == 0, core, 1 - core)
        token = (2 * ((f // 8) % nch) + side) * 8 + f % 8
        keep = token <= 8 * me + iota((64, count), 0) % 8

        def pick(at):
            own = kvg[:, 16 * at : 16 * at + 16, :].astype(F32)
            pair = kvp[:, 16 * at : 16 * at + 16, :].astype(F32)
            both = [
                jnp.where(g == 0, a[:, 0:8, :], a[:, 8:16, :]).reshape(8 * nch, HD) for a in (own, pair)
            ]
            return jnp.concatenate(both, 0).astype(BF16)

        s = jnp.where(keep, dot_t(qg[g, chip], pick(0)), -1e30)
        m = jnp.max(s, axis=1, keepdims=True)
        p = jnp.exp2((s - m) * SCALE)
        total = jnp.sum(p, axis=1, keepdims=True)
        lam = jnp.broadcast_to(m * SCALE + jnp.log2(total), (64, HD))
        return dot(p.astype(BF16), pick(1)) / total, as_row(lam)

    def spot(share):
        hi = share.astype(BF16).astype(F32)
        return jnp.where(twice, jnp.where(first, hi, share - hi), 0.0).astype(BF16)

    def merge_half(g):
        own, own_lam = self_half(g)
        partials(g).wait_recv()
        stat = rs_r[g, :, 64:80, :].astype(F32)
        lam = stat[:, 0, :] + stat[:, 1, :] + stat[:, 2, :]
        peak = jnp.maximum(jnp.max(lam, axis=0, keepdims=True), own_lam)
        share = jnp.exp2(lam - peak)
        own_share = jnp.exp2(own_lam - peak)
        total = jnp.sum(share, axis=0, keepdims=True) + own_share
        share = share / total
        own = own.astype(BF16)
        acc = dot(spot(own_share / total), jnp.concatenate([own, own], 0))
        for j in range(0, nch, 2):
            left = jnp.concatenate([spot(share[j : j + 1]), spot(share[j + 1 : j + 2])], 1)
            a, b = rs_r[g, j, 0:64, :], rs_r[g, j + 1, 0:64, :]
            acc = acc + dot(left, jnp.concatenate([a, a, b, b], 0))
        ag[g, pl.ds(chip, 1)] = acc.astype(BF16)[None]
        merged(g).start()

    rows = 8 * nch
    part = rows // ntp

    def tp_copy(i, c):
        t = (tp + 1 + i) % ntp if c == 0 else (tp + i) % ntp
        where = {"tp": t} if c == 0 else {"tp": t, "ctx": partner}
        return remote(tp_s.at[c, t], tp_r.at[c, tp], tp_ss.at[c, i], tp_rs.at[c, tp], **where)

    def project():
        merged(0).wait_recv()
        merged(1).wait_recv()
        w_c.wait_recv()
        lw.wait()
        parts = [jnp.zeros((rows, w_v.shape[1]), F32)] * 2
        for hp in range(8):
            both = ag[hp // 4, :, 16 * (hp % 4) : 16 * (hp % 4) + 16, :].astype(F32)
            a = jnp.concatenate([both[:, 0:8, :].reshape(rows, HD), both[:, 8:16, :].reshape(rows, HD)], 1)
            for c, w in enumerate((w_v, pw_v)):
                parts[c] = parts[c] + dot(a.astype(BF16), w[hp * 2 * HD : (hp + 1) * 2 * HD, :])
        for c in range(2):
            for t in range(ntp):
                tp_s[c, t] = parts[c][t * part : (t + 1) * part].astype(BF16)
        loop(ntp - 1, lambda i: tp_copy(i, 0).start())
        loop(ntp, lambda i: tp_copy(i, 1).start())

    def anchor_step(j):
        pl.when(j == 1)(lambda: merge_half(0))
        pl.when(j == 2)(lambda: merge_half(1))
        pl.when(j == 3)(lambda: anchor_in(1))
        pl.when(j == 4)(out0.start)
        pl.when(j == 5)(project)
        h = 2 * j

        @pl.when(me != 0)
        def _():
            b_scores(h + 1, 1)
            b_soft(h, 0)
            b_mix(h, 0)
            b_scores(jnp.minimum(h + 2, 15), 0)
            b_soft(h + 1, 1)
            b_mix(h + 1, 1)

        @pl.when(me == 0)
        def _():
            for k in (h, h + 1):
                value = st_o[k, :, 0:HD] / st_o[k, :, HD:]
                out_v[:, pl.ds(pl.multiple_of(k * HD, HD), HD)] = value.astype(BF16)

    kv_c.wait_recv()
    anchor_in(0)
    b_scores(0, 0)
    loop(8, anchor_step)
    out1.start()

    def tp_recv(c, t):
        buf = tp_r.at[c, t]
        where = {"tp": t} if c == 0 else {"tp": t, "ctx": partner}
        remote(buf, buf, tp_ss.at[c, 0], tp_rs.at[c, t], **where).wait_recv()

    loop(ntp - 1, lambda i: tp_recv(0, (tp + 1 + i) % ntp))
    loop(ntp, lambda i: tp_recv(1, i))
    tp_r[0, pl.ds(tp, 1)] = tp_s[0, pl.ds(tp, 1)]
    mine_sum = jnp.sum(tp_r[0].astype(F32), axis=0)
    pair_sum = jnp.sum(tp_r[1].astype(F32), axis=0)
    groups = part // 8
    even = jnp.where(core == 0, mine_sum, pair_sum).reshape(groups, 1, 8, -1)
    odd = jnp.where(core == 0, pair_sum, mine_sum).reshape(groups, 1, 8, -1)
    query_out[...] = jnp.concatenate([even, odd], 1).reshape(2 * part, -1).astype(BF16)

    def sent(g):
        for spread in (queries(g), anchors(g), partials(g), merged(g)):
            spread.wait_send()
        anchor_pair(g).wait_send()

        @pl.when(me == 0)
        def _():
            scatter_copies(g, 0)[1].wait_send()

            def step(i):
                ck, cv = scatter_copies(g, 1 + i)
                ck.wait_send()
                cv.wait_send()

            loop(nch - 1, step)

    loop(2, sent)
    query_kv.wait_send()
    loop(ntp - 1, lambda i: tp_copy(i, 0).wait_send())
    loop(ntp, lambda i: tp_copy(i, 1).wait_send())
    for c in (pk_c, pv_c, kv_c, w_c):
        c.wait_send()
    out0.wait()
    out1.wait()


def an_view(ref, nch, piece):
    return ref.reshape(nch, piece, ref.shape[-1])


def body(nch, ntp, ctx_q, ctx_k, ctx_v, query_q, query_k, query_v, weight):
    blk, width = ctx_q.shape
    cols = ctx_k.shape[1]
    tq = blk // 3
    piece = blk // nch
    part = 8 * nch // ntp
    vmem = pltpu.VMEM
    dma = pltpu.SemaphoreType.DMA
    scratch = [
        vmem((blk, width), BF16), vmem((blk, cols), BF16), vmem((blk, cols), BF16), vmem(weight.shape, BF16),
        vmem((blk, cols), BF16), vmem((blk, cols), BF16), vmem(weight.shape, BF16), vmem((blk, width), BF16),
        vmem((2, blk, 2 * HD), BF16), vmem((2, blk, 2 * HD), BF16), vmem((2, blk, 2 * HD), BF16),
        vmem((2, nch, 64, HD), BF16), vmem((nch, 32, HD), BF16), vmem((nch, 32, HD), BF16),
        vmem((2, 2, nch, piece, HD), BF16),
        vmem((2, nch, 80, HD), BF16), vmem((2, nch, 80, HD), BF16), vmem((nch, 8, HD), F32),
        vmem((2, nch, 64, HD), BF16), vmem((2, ntp, part, weight.shape[1]), BF16), vmem((2, ntp, part, weight.shape[1]), BF16),
        vmem((16, blk, 2 * HD), F32), vmem((16, blk, HD), F32),
    ]
    scratch += [vmem((2 * tq, tq * i), F32) for i in (1, 2, 3)] + [vmem((2 * tq, tq * i), BF16) for i in (1, 2, 3)]
    scratch += [vmem((blk, blk), F32)] * 2 + [vmem((blk, blk), BF16)] * 2
    scratch += [vmem((256, 2 * blk), F32)] * 2 + [vmem((256, 2 * blk), BF16)] * 2 + [vmem((256, HD), F32)] * 2
    scratch += [
        dma((9,)), dma((6,)), dma((6,)), dma((9, nch)), dma((9, nch)), dma((2, 2, nch)), dma((2,)),
        dma((2, ntp)), dma((2, ntp)),
    ]
    hbm = pl.BlockSpec(memory_space=pl.ANY)
    near = pl.BlockSpec(memory_space=pltpu.VMEM)
    return pl.pallas_call(
        functools.partial(kernel, nch, ntp, blk),
        out_shape=(
            jax.ShapeDtypeStruct((blk, width), BF16),
            jax.ShapeDtypeStruct((2 * part, weight.shape[1]), BF16),
        ),
        in_specs=[hbm, hbm, hbm, near, near, near, hbm],
        out_specs=(hbm, near),
        scratch_shapes=scratch,
        compiler_params=pltpu.CompilerParams(
            collective_id=0, has_side_effects=True, vmem_limit_bytes=62 * 2**20
        ),
        name="star",
    )(
        ctx_q, ctx_k.reshape(nch, piece, cols), ctx_v.reshape(nch, piece, cols),
        query_q, query_k, query_v, weight,
    )


def solution(mesh):
    nch, ntp = mesh.shape["ctx"] // 2, mesh.shape["tp"]
    return jax.shard_map(
        functools.partial(body, nch, ntp),
        mesh=mesh,
        in_specs=(P("ctx", "tp"),) * 6 + (P("tp", "ctx"),),
        out_specs=(P("ctx", "tp"), P("tp", "ctx")),
        check_vma=False,
    )
```

```python
import functools
import math

import jax
import jax.numpy as jnp
from jax import lax
from jax.experimental import pallas as pl
from jax.experimental.pallas import tpu as pltpu
from jax.sharding import PartitionSpec as P

HD = 128
SCALE = HD**-0.5 * math.log2(math.e)
F32 = jnp.float32
BF16 = jnp.bfloat16
MESH = pl.DeviceIdType.MESH
CHUNK = 16


def dot(a, b):
    return jnp.dot(a, b, preferred_element_type=F32)


def dot_t(a, b):
    return lax.dot_general(a, b, (((1,), (1,)), ((), ())), preferred_element_type=F32)


def iota(shape, dim):
    return lax.broadcasted_iota(jnp.int32, shape, dim)


def loop(count, step):
    def body(i, carry):
        step(i)
        return carry

    lax.fori_loop(0, count, body, 0)


def kernel(
    nch, ntp, blk,
    ctx_q, ctx_k, ctx_v, query_q, query_k, query_v, weight,
    ctx_out, query_out,
    q_v, k_v, v_v, w_v, pk_v, pv_v, pw_v, out_v,
    vv_own, vv_pair, vv_anchor,
    qg, kvg, kvp, an, rs_s, rs_r, lam_v, ag, tp_s, tp_r,
    st_o, st_m,
    sa0, sa1, sa2, pa0, pa1, pa2, sb0, sb1, pb0, pb1, sq0, sq1, pq0, pq1, mq0, mq1,
    loc, pair_s, pair_r, ex_s, ex_r, sc_s, pc_r, tp_ss, tp_rs,
):
    me = lax.axis_index("ctx")
    tp = lax.axis_index("tp")
    chip = me // 2
    core = me % 2
    partner = me + 1 - 2 * core
    tq = blk // 3
    piece = blk // nch

    def local(i, src, dst):
        return pltpu.make_async_copy(src, dst, loc.at[i])

    def half_cols(g):
        return pl.ds(pl.multiple_of(g * HD, HD), HD)

    lk = local(0, ctx_k, an_view(k_v, nch, piece))
    lv = local(1, ctx_v, an_view(v_v, nch, piece))
    lw = local(2, weight, w_v)

    def strip(i):
        return pl.ds(pl.multiple_of(i * 2 * HD, 2 * HD), 2 * HD)

    def queries_in(i):
        return local(5 + i, ctx_q.at[:, strip(i)], q_v.at[:, strip(i)])

    def result_out(i):
        return local(13 + i, out_v.at[:, strip(i)], ctx_out.at[:, strip(i)])

    def first_key(g):
        return pltpu.make_async_copy(ctx_k.at[0, :, half_cols(g)], an.at[0, g, 0], loc.at[3 + g])

    lk.start()
    lv.start()
    loop(8, lambda i: queries_in(i).start())

    barrier = pltpu.get_barrier_semaphore()

    def greet(**where):
        pl.semaphore_signal(barrier, inc=1, device_id=where, device_id_type=MESH)

    loop(nch - 1, lambda i: greet(ctx=2 * ((chip + 1 + i) % nch) + core))
    greet(ctx=partner)

    def greet_tp(i):
        greet(tp=(tp + 1 + i) % ntp)
        greet(tp=(tp + 1 + i) % ntp, ctx=partner)

    loop(ntp - 1, greet_tp)

    @pl.when(me == 0)
    def _():
        loop(nch - 1, lambda i: greet(ctx=2 * (1 + i) + 1))

    @pl.when((core == 1) & (chip > 0))
    def _():
        greet(ctx=0)

    x = query_q[...].astype(F32)
    for g in range(2):
        rows = [x[:, h * HD : (h + 1) * HD] for h in range(8 * g, 8 * g + 8)]
        qg[g, chip] = jnp.concatenate(rows, 0).astype(BF16)
    xk = query_k[...].astype(F32)
    xv = query_v[...].astype(F32)
    kvg[chip] = jnp.concatenate([xk[:, :HD], xk[:, HD:], xv[:, :HD], xv[:, HD:]], 0).astype(BF16)

    def remote(src, dst, send, recv, **where):
        return pltpu.make_async_remote_copy(
            src_ref=src, dst_ref=dst, send_sem=send, recv_sem=recv, device_id=where, device_id_type=MESH
        )

    def pair_copy(i, src, dst):
        return remote(src, dst, pair_s.at[i], pair_r.at[i], ctx=partner)

    class Spread:
        def __init__(self, index, src, dst):
            self.index, self.src, self.dst = index, src, dst

        def copy(self, i):
            j = (chip + 1 + i) % nch
            send, recv = ex_s.at[self.index, i], ex_r.at[self.index, chip]
            return remote(self.src(j), self.dst(chip), send, recv, ctx=2 * j + core)

        def start(self):
            loop(nch - 1, lambda i: self.copy(i).start())

        def wait_send(self):
            loop(nch - 1, lambda i: self.copy(i).wait_send())

        def wait_recv(self):
            def step(i):
                j = (chip + 1 + i) % nch
                buf = self.dst(j)
                remote(buf, buf, ex_s.at[self.index, i], ex_r.at[self.index, j], ctx=2 * j + core).wait_recv()

            loop(nch - 1, step)

    def queries(g):
        return Spread(g, lambda j: qg.at[g, chip], lambda c: qg.at[g, c])

    def anchors(g):
        return Spread(2 + g, lambda j: an.at[core, g, chip], lambda c: an.at[core, g, c])

    def partials(g):
        return Spread(4 + g, lambda j: rs_s.at[g, j], lambda c: rs_r.at[g, c])

    def merged(g):
        return Spread(6 + g, lambda j: ag.at[g, chip], lambda c: ag.at[g, c])

    query_kv = Spread(8, lambda j: kvg.at[chip], lambda c: kvg.at[c])

    def scatter_copies(g, j):
        ck = remote(ctx_k.at[j, :, half_cols(g)], an.at[0, g, j], sc_s.at[g, 0, j], pc_r.at[g], ctx=2 * j)
        cv = remote(ctx_v.at[j, :, half_cols(g)], an.at[1, g, j], sc_s.at[g, 1, j], pc_r.at[g], ctx=2 * j + 1)
        return ck, cv

    def scatter(g):
        @pl.when(me == 0)
        def _():
            first_key(g).start()
            scatter_copies(g, 0)[1].start()

            def step(i):
                ck, cv = scatter_copies(g, 1 + i)
                ck.start()
                cv.start()

            loop(nch - 1, step)

    pk_c = pair_copy(0, ctx_k, an_view(pk_v, nch, piece))
    pv_c = pair_copy(1, ctx_v, an_view(pv_v, nch, piece))
    kv_c = pair_copy(2, kvg, kvp)
    w_c = pair_copy(3, weight, pw_v)

    def anchor_pair(g):
        return pair_copy(4 + g, an.at[core, g], an.at[core, g])

    def begin():
        extra = jnp.where(me == 0, nch - 1, jnp.where((core == 1) & (chip > 0), 1, 0))
        pl.semaphore_wait(barrier, nch - 1 + 1 + 2 * (ntp - 1) + extra)
        queries(0).start()
        scatter(0)
        pk_c.start()
        pv_c.start()
        queries(1).start()
        scatter(1)
        query_kv.start()

    def hand_on(g):
        @pl.when(me == 0)
        def _():
            first_key(g).wait()

        @pl.when(me != 0)
        def _():
            own = an.at[core, g, chip]
            remote(own, own, sc_s.at[g, 0, 0], pc_r.at[g], ctx=partner).wait_recv()

        anchors(g).start()

    def fill(vv, v):
        for g in range(2):
            vv[g, :, 0:HD] = v[:, g * HD : (g + 1) * HD]
            vv[g, :, HD:] = jnp.ones((blk, HD), BF16)

    s_a, p_a = (sa0, sa1, sa2), (pa0, pa1, pa2)

    def a_scores(hp, i):
        n = tq * (i + 1)
        q = q_v[i * tq : n, pl.ds(pl.multiple_of(hp * 2 * HD, 2 * HD), 2 * HD)]
        q = jnp.concatenate([q[:, :HD], q[:, HD:]], 0)
        s_a[i][...] = dot_t(q, k_v[0:n, half_cols(hp // 4)])

    def a_soft(hp, i):
        n = tq * (i + 1)
        for r in range(2 * tq // CHUNK):
            low = r * CHUNK
            s = s_a[i][low : low + CHUNK, :]
            keep = iota((CHUNK, tq), 1) <= iota((CHUNK, tq), 0) + low % tq
            d = jnp.where(keep, s[:, n - tq :], -1e30)
            s = d if i == 0 else jnp.concatenate([s[:, : n - tq], d], 1)
            m = jnp.max(s, axis=1, keepdims=True)
            p_a[i][low : low + CHUNK, :] = jnp.exp2((s - m) * SCALE).astype(BF16)
            at = i * tq + low % tq
            st_m[2 * hp + low // tq, at : at + CHUNK, :] = jnp.broadcast_to(m, (CHUNK, HD))

    def a_mix(hp, i):
        n = tq * (i + 1)
        o = dot(p_a[i][...], vv_own[hp // 4, 0:n, :])
        st_o[2 * hp, i * tq : n, :] = o[:tq]
        st_o[2 * hp + 1, i * tq : n, :] = o[tq:]

    s_q, p_q, m_q = (sq0, sq1), (pq0, pq1), (mq0, mq1)
    per_g = nch // 4

    def q_scores(g, t, b):
        q = qg[g, pl.ds(4 * t, 4)].reshape(256, HD)
        s_q[b][:, 0:blk] = dot_t(q, k_v[:, half_cols(g)])
        s_q[b][:, blk:] = dot_t(q, pk_v[:, half_cols(g)])

    def q_soft(b):
        for r in range(256 // CHUNK):
            rows = slice(r * CHUNK, (r + 1) * CHUNK)
            s = s_q[b][rows, :]
            m = jnp.max(s, axis=1, keepdims=True)
            p_q[b][rows, :] = jnp.exp2((s - m) * SCALE).astype(BF16)
            m_q[b][rows, :] = jnp.broadcast_to(m, (CHUNK, HD))

    twice = iota((64, HD), 1) % 64 == iota((64, HD), 0)
    first = iota((1, HD), 1) < 64

    def as_row(column):
        return jnp.sum(jnp.where(twice, column, 0.0), axis=0, keepdims=True)

    def q_mix(g, t, b):
        o = dot(p_q[b][:, 0:blk], vv_own[g]) + dot(p_q[b][:, blk:], vv_pair[g])
        total = o[:, HD:]
        lam = m_q[b][...] * SCALE + jnp.log2(total)
        o = (o[:, :HD] / total).astype(BF16)
        for u in range(4):
            rs_s[g, 4 * t + u, 0:64, :] = o[u * 64 : (u + 1) * 64]
            lam_v[4 * t + u, 0:1, :] = as_row(lam[u * 64 : (u + 1) * 64])

    def query_half(g):
        queries(g).wait_recv()

        @pl.when(g == 0)
        def _():
            pk_c.wait_recv()
            pv_c.wait_recv()
            fill(vv_pair, pv_v)

        q_scores(g, 0, 0)

        def step(j):
            q_scores(g, 2 * j + 1, 1)
            q_soft(0)
            q_mix(g, 2 * j, 0)
            q_scores(g, jnp.minimum(2 * j + 2, per_g - 1), 0)
            q_soft(1)
            q_mix(g, 2 * j + 1, 1)

        loop(per_g // 2, step)
        lam = lam_v[:, 0:1, :]
        hi = lam.astype(BF16).astype(F32)
        mid = (lam - hi).astype(BF16).astype(F32)
        row = iota((nch, 16, HD), 1)
        stats = jnp.where(row == 0, hi, jnp.where(row == 1, mid, jnp.where(row == 2, lam - hi - mid, 0.0)))
        rs_s[g, :, 64:80, :] = stats.astype(BF16)
        partials(g).start()
        hand_on(g)
        rs_r[g, pl.ds(chip, 1)] = rs_s[g, pl.ds(chip, 1)]

    def anchors_across(g):
        anchors(g).wait_recv()
        anchor_pair(g).start()

    early = (114 - 7 * tp - 9 * (chip // 4) - 18 * (chip % 4)) // 28
    early = jnp.maximum(0, jnp.minimum(4, early))
    at_query = jnp.maximum(4, early + 1)

    lk.wait()
    lv.wait()
    fill(vv_own, v_v)
    queries_in(0).wait()
    a_scores(0, 0)

    def own_step(j):
        @pl.when((j > 0) & (j < 8))
        def _():
            queries_in(j).wait()

        @pl.when(j > 0)
        def _():
            hp = j - 1
            a_scores(hp, 1)
            a_soft(hp, 0)
            a_mix(hp, 0)
            a_scores(hp, 2)
            a_soft(hp, 1)
            a_mix(hp, 1)
            a_scores(jnp.minimum(hp + 1, 7), 0)
            a_soft(hp, 2)
            a_mix(hp, 2)

        pl.when(j == early)(begin)
        @pl.when(j == at_query)
        def _():
            loop(2, query_half)
            query_kv.wait_recv()
            kv_c.start()
            w_c.start()
            lw.start()

        pl.when(j == 7)(lambda: anchors_across(0))

    loop(9, own_step)

    s_b, p_b = (sb0, sb1), (pb0, pb1)

    def b_scores(h, b):
        q = q_v[:, pl.ds(pl.multiple_of(h * HD, HD), HD)]
        s_b[b][...] = dot_t(q, an[0, h // 8].reshape(blk, HD))

    def b_soft(h, b):
        for r in range(blk // CHUNK):
            rows = slice(r * CHUNK, (r + 1) * CHUNK)
            s = s_b[b][rows, :]
            old = st_m[h, rows, :]
            m = jnp.maximum(jnp.max(s, axis=1, keepdims=True), old[:, 0:1])
            p_b[b][rows, :] = jnp.exp2((s - m) * SCALE).astype(BF16)
            st_m[h, rows, :] = jnp.exp2((old - m) * SCALE)

    def b_mix(h, b):
        o = dot(p_b[b][...], vv_anchor[h // 8])
        factor = st_m[h]
        top = factor * st_o[h, :, 0:HD] + o[:, :HD]
        total = factor * st_o[h, :, HD:] + o[:, HD:]
        out_v[:, pl.ds(pl.multiple_of(h * HD, HD), HD)] = (top / total).astype(BF16)

    def anchor_in(g):
        other = an.at[1 - core, g]
        remote(other, other, pair_s.at[4 + g], pair_r.at[4 + g], ctx=partner).wait_recv()
        vv_anchor[g, :, 0:HD] = an[1, g].reshape(blk, HD)
        vv_anchor[g, :, HD:] = jnp.ones((blk, HD), BF16)

    def self_half(g):
        count = 16 * nch
        f = iota((64, count), 1)
        side = jnp.where(f // (8 * nch) == 0, core, 1 - core)
        token = (2 * ((f // 8) % nch) + side) * 8 + f % 8
        keep = token <= 8 * me + iota((64, count), 0) % 8

        def pick(at):
            own = kvg[:, 16 * at : 16 * at + 16, :].astype(F32)
            pair = kvp[:, 16 * at : 16 * at + 16, :].astype(F32)
            both = [
                jnp.where(g == 0, a[:, 0:8, :], a[:, 8:16, :]).reshape(8 * nch, HD) for a in (own, pair)
            ]
            return jnp.concatenate(both, 0).astype(BF16)

        s = jnp.where(keep, dot_t(qg[g, chip], pick(0)), -1e30)
        m = jnp.max(s, axis=1, keepdims=True)
        p = jnp.exp2((s - m) * SCALE)
        total = jnp.sum(p, axis=1, keepdims=True)
        lam = jnp.broadcast_to(m * SCALE + jnp.log2(total), (64, HD))
        return dot(p.astype(BF16), pick(1)) / total, as_row(lam)

    def spot(share):
        hi = share.astype(BF16).astype(F32)
        return jnp.where(twice, jnp.where(first, hi, share - hi), 0.0).astype(BF16)

    def merge_half(g):
        own, own_lam = self_half(g)
        partials(g).wait_recv()
        stat = rs_r[g, :, 64:80, :].astype(F32)
        lam = stat[:, 0, :] + stat[:, 1, :] + stat[:, 2, :]
        peak = jnp.maximum(jnp.max(lam, axis=0, keepdims=True), own_lam)
        share = jnp.exp2(lam - peak)
        own_share = jnp.exp2(own_lam - peak)
        total = jnp.sum(share, axis=0, keepdims=True) + own_share
        share = share / total
        own = own.astype(BF16)
        acc = dot(spot(own_share / total), jnp.concatenate([own, own], 0))
        for j in range(0, nch, 2):
            left = jnp.concatenate([spot(share[j : j + 1]), spot(share[j + 1 : j + 2])], 1)
            a, b = rs_r[g, j, 0:64, :], rs_r[g, j + 1, 0:64, :]
            acc = acc + dot(left, jnp.concatenate([a, a, b, b], 0))
        ag[g, pl.ds(chip, 1)] = acc.astype(BF16)[None]
        merged(g).start()

    rows = 8 * nch
    part = rows // ntp

    def tp_copy(i, c):
        t = (tp + 1 + i) % ntp if c == 0 else (tp + i) % ntp
        where = {"tp": t} if c == 0 else {"tp": t, "ctx": partner}
        return remote(tp_s.at[c, t], tp_r.at[c, tp], tp_ss.at[c, i], tp_rs.at[c, tp], **where)

    def project():
        merged(0).wait_recv()
        merged(1).wait_recv()
        w_c.wait_recv()
        lw.wait()
        parts = [jnp.zeros((rows, w_v.shape[1]), F32)] * 2
        for hp in range(8):
            both = ag[hp // 4, :, 16 * (hp % 4) : 16 * (hp % 4) + 16, :].astype(F32)
            a = jnp.concatenate([both[:, 0:8, :].reshape(rows, HD), both[:, 8:16, :].reshape(rows, HD)], 1)
            for c, w in enumerate((w_v, pw_v)):
                parts[c] = parts[c] + dot(a.astype(BF16), w[hp * 2 * HD : (hp + 1) * 2 * HD, :])
        for c in range(2):
            for t in range(ntp):
                tp_s[c, t] = parts[c][t * part : (t + 1) * part].astype(BF16)
        loop(ntp - 1, lambda i: tp_copy(i, 0).start())
        loop(ntp, lambda i: tp_copy(i, 1).start())

    def anchor_step(j):
        @pl.when(j == 0)
        def _():
            kv_c.wait_recv()
            merge_half(0)

        pl.when(j == 1)(lambda: merge_half(1))
        pl.when(j == 1)(lambda: anchors_across(1))
        pl.when(j == 3)(lambda: anchor_in(1))
        pl.when(j == 4)(project)
        h = 2 * j

        @pl.when(me != 0)
        def _():
            b_scores(h + 1, 1)
            b_soft(h, 0)
            b_mix(h, 0)
            b_scores(jnp.minimum(h + 2, 15), 0)
            b_soft(h + 1, 1)
            b_mix(h + 1, 1)

        @pl.when(me == 0)
        def _():
            for k in (h, h + 1):
                value = st_o[k, :, 0:HD] / st_o[k, :, HD:]
                out_v[:, pl.ds(pl.multiple_of(k * HD, HD), HD)] = value.astype(BF16)

        result_out(j).start()

    anchor_in(0)
    b_scores(0, 0)
    loop(8, anchor_step)

    def tp_recv(c, t):
        buf = tp_r.at[c, t]
        where = {"tp": t} if c == 0 else {"tp": t, "ctx": partner}
        remote(buf, buf, tp_ss.at[c, 0], tp_rs.at[c, t], **where).wait_recv()

    loop(ntp - 1, lambda i: tp_recv(0, (tp + 1 + i) % ntp))
    loop(ntp, lambda i: tp_recv(1, i))
    tp_r[0, pl.ds(tp, 1)] = tp_s[0, pl.ds(tp, 1)]
    mine_sum = jnp.sum(tp_r[0].astype(F32), axis=0)
    pair_sum = jnp.sum(tp_r[1].astype(F32), axis=0)
    groups = part // 8
    even = jnp.where(core == 0, mine_sum, pair_sum).reshape(groups, 1, 8, -1)
    odd = jnp.where(core == 0, pair_sum, mine_sum).reshape(groups, 1, 8, -1)
    query_out[...] = jnp.concatenate([even, odd], 1).reshape(2 * part, -1).astype(BF16)

    def sent(g):
        for spread in (queries(g), anchors(g), partials(g), merged(g)):
            spread.wait_send()
        anchor_pair(g).wait_send()

        @pl.when(me == 0)
        def _():
            scatter_copies(g, 0)[1].wait_send()

            def step(i):
                ck, cv = scatter_copies(g, 1 + i)
                ck.wait_send()
                cv.wait_send()

            loop(nch - 1, step)

    loop(2, sent)
    query_kv.wait_send()
    loop(ntp - 1, lambda i: tp_copy(i, 0).wait_send())
    loop(ntp, lambda i: tp_copy(i, 1).wait_send())
    for c in (pk_c, pv_c, kv_c, w_c):
        c.wait_send()
    loop(8, lambda i: result_out(i).wait())


def an_view(ref, nch, piece):
    return ref.reshape(nch, piece, ref.shape[-1])


def body(nch, ntp, ctx_q, ctx_k, ctx_v, query_q, query_k, query_v, weight):
    blk, width = ctx_q.shape
    cols = ctx_k.shape[1]
    tq = blk // 3
    piece = blk // nch
    part = 8 * nch // ntp
    vmem = pltpu.VMEM
    dma = pltpu.SemaphoreType.DMA
    scratch = [
        vmem((blk, width), BF16), vmem((blk, cols), BF16), vmem((blk, cols), BF16), vmem(weight.shape, BF16),
        vmem((blk, cols), BF16), vmem((blk, cols), BF16), vmem(weight.shape, BF16), vmem((blk, width), BF16),
        vmem((2, blk, 2 * HD), BF16), vmem((2, blk, 2 * HD), BF16), vmem((2, blk, 2 * HD), BF16),
        vmem((2, nch, 64, HD), BF16), vmem((nch, 32, HD), BF16), vmem((nch, 32, HD), BF16),
        vmem((2, 2, nch, piece, HD), BF16),
        vmem((2, nch, 80, HD), BF16), vmem((2, nch, 80, HD), BF16), vmem((nch, 8, HD), F32),
        vmem((2, nch, 64, HD), BF16), vmem((2, ntp, part, weight.shape[1]), BF16), vmem((2, ntp, part, weight.shape[1]), BF16),
        vmem((16, blk, 2 * HD), F32), vmem((16, blk, HD), F32),
    ]
    scratch += [vmem((2 * tq, tq * i), F32) for i in (1, 2, 3)] + [vmem((2 * tq, tq * i), BF16) for i in (1, 2, 3)]
    scratch += [vmem((blk, blk), F32)] * 2 + [vmem((blk, blk), BF16)] * 2
    scratch += [vmem((256, 2 * blk), F32)] * 2 + [vmem((256, 2 * blk), BF16)] * 2 + [vmem((256, HD), F32)] * 2
    scratch += [
        dma((21,)), dma((6,)), dma((6,)), dma((9, nch)), dma((9, nch)), dma((2, 2, nch)), dma((2,)),
        dma((2, ntp)), dma((2, ntp)),
    ]
    hbm = pl.BlockSpec(memory_space=pl.ANY)
    near = pl.BlockSpec(memory_space=pltpu.VMEM)
    return pl.pallas_call(
        functools.partial(kernel, nch, ntp, blk),
        out_shape=(
            jax.ShapeDtypeStruct((blk, width), BF16),
            jax.ShapeDtypeStruct((2 * part, weight.shape[1]), BF16),
        ),
        in_specs=[hbm, hbm, hbm, near, near, near, hbm],
        out_specs=(hbm, near),
        scratch_shapes=scratch,
        compiler_params=pltpu.CompilerParams(
            collective_id=0, has_side_effects=True, vmem_limit_bytes=62 * 2**20
        ),
        name="star",
    )(
        ctx_q, ctx_k.reshape(nch, piece, cols), ctx_v.reshape(nch, piece, cols),
        query_q, query_k, query_v, weight,
    )


def solution(mesh):
    nch, ntp = mesh.shape["ctx"] // 2, mesh.shape["tp"]
    return jax.shard_map(
        functools.partial(body, nch, ntp),
        mesh=mesh,
        in_specs=(P("ctx", "tp"),) * 6 + (P("tp", "ctx"),),
        out_specs=(P("ctx", "tp"), P("tp", "ctx")),
        check_vma=False,
    )
```

```python
import functools
import math

import jax
import jax.numpy as jnp
from jax import lax
from jax.experimental import pallas as pl
from jax.experimental.pallas import tpu as pltpu
from jax.sharding import PartitionSpec as P

HD = 128
SCALE = HD**-0.5 * math.log2(math.e)
F32 = jnp.float32
BF16 = jnp.bfloat16
MESH = pl.DeviceIdType.MESH
CHUNK = 16


def dot(a, b):
    return jnp.dot(a, b, preferred_element_type=F32)


def dot_t(a, b):
    return lax.dot_general(a, b, (((1,), (1,)), ((), ())), preferred_element_type=F32)


def iota(shape, dim):
    return lax.broadcasted_iota(jnp.int32, shape, dim)


def loop(count, step):
    def body(i, carry):
        step(i)
        return carry

    lax.fori_loop(0, count, body, 0)


def kernel(
    nch, ntp, blk,
    ctx_q, ctx_k, ctx_v, query_q, query_k, query_v, weight,
    ctx_out, query_out,
    q_v, k_v, v_v, w_v, pk_v, pv_v, pw_v, out_v,
    vv_own, vv_pair, vv_anchor,
    qg, kvg, kvp, an, rs_s, rs_r, lam_v, ag, tp_s, tp_r,
    st_o, st_m,
    sa0, sa1, sa2, pa0, pa1, pa2, sb0, sb1, pb0, pb1, sq0, sq1, pq0, pq1, mq0, mq1,
    loc, pair_s, pair_r, ex_s, ex_r, sc_s, pc_r, tp_ss, tp_rs,
):
    me = lax.axis_index("ctx")
    tp = lax.axis_index("tp")
    chip = me // 2
    core = me % 2
    partner = me + 1 - 2 * core
    tq = blk // 3
    piece = blk // nch

    def local(i, src, dst):
        return pltpu.make_async_copy(src, dst, loc.at[i])

    def half_cols(g):
        return pl.ds(pl.multiple_of(g * HD, HD), HD)

    lk = local(0, ctx_k, an_view(k_v, nch, piece))
    lv = local(1, ctx_v, an_view(v_v, nch, piece))
    lw = local(2, weight, w_v)

    def strip(i):
        return pl.ds(pl.multiple_of(i * 2 * HD, 2 * HD), 2 * HD)

    def queries_in(i):
        return local(5 + i, ctx_q.at[:, strip(i)], q_v.at[:, strip(i)])

    def result_out(i):
        return local(13 + i, out_v.at[:, strip(i)], ctx_out.at[:, strip(i)])

    def first_key(g):
        return pltpu.make_async_copy(ctx_k.at[0, :, half_cols(g)], an.at[0, g, 0], loc.at[3 + g])

    lk.start()
    lv.start()
    loop(8, lambda i: queries_in(i).start())

    barrier = pltpu.get_barrier_semaphore()

    def greet(**where):
        pl.semaphore_signal(barrier, inc=1, device_id=where, device_id_type=MESH)

    loop(nch - 1, lambda i: greet(ctx=2 * ((chip + 1 + i) % nch) + core))
    greet(ctx=partner)

    def greet_tp(i):
        greet(tp=(tp + 1 + i) % ntp)
        greet(tp=(tp + 1 + i) % ntp, ctx=partner)

    loop(ntp - 1, greet_tp)

    @pl.when(me == 0)
    def _():
        loop(nch - 1, lambda i: greet(ctx=2 * (1 + i) + 1))

    @pl.when((core == 1) & (chip > 0))
    def _():
        greet(ctx=0)

    x = query_q[...].astype(F32)
    for g in range(2):
        rows = [x[:, h * HD : (h + 1) * HD] for h in range(8 * g, 8 * g + 8)]
        qg[g, chip] = jnp.concatenate(rows, 0).astype(BF16)
    xk = query_k[...].astype(F32)
    xv = query_v[...].astype(F32)
    kvg[chip] = jnp.concatenate([xk[:, :HD], xk[:, HD:], xv[:, :HD], xv[:, HD:]], 0).astype(BF16)

    def remote(src, dst, send, recv, **where):
        return pltpu.make_async_remote_copy(
            src_ref=src, dst_ref=dst, send_sem=send, recv_sem=recv, device_id=where, device_id_type=MESH
        )

    def pair_copy(i, src, dst):
        return remote(src, dst, pair_s.at[i], pair_r.at[i], ctx=partner)

    class Spread:
        def __init__(self, index, src, dst):
            self.index, self.src, self.dst = index, src, dst

        def copy(self, i):
            j = (chip + 1 + i) % nch
            send, recv = ex_s.at[self.index, i], ex_r.at[self.index, chip]
            return remote(self.src(j), self.dst(chip), send, recv, ctx=2 * j + core)

        def start(self):
            loop(nch - 1, lambda i: self.copy(i).start())

        def wait_send(self):
            loop(nch - 1, lambda i: self.copy(i).wait_send())

        def wait_recv(self):
            def step(i):
                j = (chip + 1 + i) % nch
                buf = self.dst(j)
                remote(buf, buf, ex_s.at[self.index, i], ex_r.at[self.index, j], ctx=2 * j + core).wait_recv()

            loop(nch - 1, step)

    def queries(g):
        return Spread(g, lambda j: qg.at[g, chip], lambda c: qg.at[g, c])

    def anchors(g):
        return Spread(2 + g, lambda j: an.at[core, g, chip], lambda c: an.at[core, g, c])

    def partials(g):
        return Spread(4 + g, lambda j: rs_s.at[g, j], lambda c: rs_r.at[g, c])

    def merged(g):
        return Spread(6 + g, lambda j: ag.at[g, chip], lambda c: ag.at[g, c])

    query_kv = Spread(8, lambda j: kvg.at[chip], lambda c: kvg.at[c])

    def scatter_copies(g, j):
        ck = remote(ctx_k.at[j, :, half_cols(g)], an.at[0, g, j], sc_s.at[g, 0, j], pc_r.at[g], ctx=2 * j)
        cv = remote(ctx_v.at[j, :, half_cols(g)], an.at[1, g, j], sc_s.at[g, 1, j], pc_r.at[g], ctx=2 * j + 1)
        return ck, cv

    def scatter(g):
        @pl.when(me == 0)
        def _():
            first_key(g).start()
            scatter_copies(g, 0)[1].start()

            def step(i):
                ck, cv = scatter_copies(g, 1 + i)
                ck.start()
                cv.start()

            loop(nch - 1, step)

    pk_c = pair_copy(0, ctx_k, an_view(pk_v, nch, piece))
    pv_c = pair_copy(1, ctx_v, an_view(pv_v, nch, piece))
    kv_c = pair_copy(2, kvg, kvp)
    w_c = pair_copy(3, weight, pw_v)

    def anchor_pair(g):
        return pair_copy(4 + g, an.at[core, g], an.at[core, g])

    def begin():
        extra = jnp.where(me == 0, nch - 1, jnp.where((core == 1) & (chip > 0), 1, 0))
        pl.semaphore_wait(barrier, nch - 1 + 1 + 2 * (ntp - 1) + extra)
        queries(0).start()
        scatter(0)
        pk_c.start()
        pv_c.start()
        queries(1).start()
        scatter(1)
        query_kv.start()

    def hand_on(g):
        @pl.when(me == 0)
        def _():
            first_key(g).wait()

        @pl.when(me != 0)
        def _():
            own = an.at[core, g, chip]
            remote(own, own, sc_s.at[g, 0, 0], pc_r.at[g], ctx=partner).wait_recv()

        anchors(g).start()

    def fill(vv, v):
        for g in range(2):
            vv[g, :, 0:HD] = v[:, g * HD : (g + 1) * HD]
            vv[g, :, HD:] = jnp.ones((blk, HD), BF16)

    s_a, p_a = (sa0, sa1, sa2), (pa0, pa1, pa2)

    def a_scores(hp, i):
        n = tq * (i + 1)
        q = q_v[i * tq : n, pl.ds(pl.multiple_of(hp * 2 * HD, 2 * HD), 2 * HD)]
        q = jnp.concatenate([q[:, :HD], q[:, HD:]], 0)
        s_a[i][...] = dot_t(q, k_v[0:n, half_cols(hp // 4)])

    def a_soft(hp, i):
        n = tq * (i + 1)
        for r in range(2 * tq // CHUNK):
            low = r * CHUNK
            s = s_a[i][low : low + CHUNK, :]
            keep = iota((CHUNK, tq), 1) <= iota((CHUNK, tq), 0) + low % tq
            d = jnp.where(keep, s[:, n - tq :], -1e30)
            s = d if i == 0 else jnp.concatenate([s[:, : n - tq], d], 1)
            m = jnp.max(s, axis=1, keepdims=True)
            p_a[i][low : low + CHUNK, :] = jnp.exp2((s - m) * SCALE).astype(BF16)
            at = i * tq + low % tq
            st_m[2 * hp + low // tq, at : at + CHUNK, :] = jnp.broadcast_to(m, (CHUNK, HD))

    def a_mix(hp, i):
        n = tq * (i + 1)
        o = dot(p_a[i][...], vv_own[hp // 4, 0:n, :])
        st_o[2 * hp, i * tq : n, :] = o[:tq]
        st_o[2 * hp + 1, i * tq : n, :] = o[tq:]

    s_q, p_q, m_q = (sq0, sq1), (pq0, pq1), (mq0, mq1)
    per_g = nch // 4

    def q_scores(g, t, b):
        q = qg[g, pl.ds(4 * t, 4)].reshape(256, HD)
        s_q[b][:, 0:blk] = dot_t(q, k_v[:, half_cols(g)])
        s_q[b][:, blk:] = dot_t(q, pk_v[:, half_cols(g)])

    def q_soft(b):
        for r in range(256 // CHUNK):
            rows = slice(r * CHUNK, (r + 1) * CHUNK)
            s = s_q[b][rows, :]
            m = jnp.max(s, axis=1, keepdims=True)
            p_q[b][rows, :] = jnp.exp2((s - m) * SCALE).astype(BF16)
            m_q[b][rows, :] = jnp.broadcast_to(m, (CHUNK, HD))

    twice = iota((64, HD), 1) % 64 == iota((64, HD), 0)
    first = iota((1, HD), 1) < 64

    def as_row(column):
        return jnp.sum(jnp.where(twice, column, 0.0), axis=0, keepdims=True)

    def q_mix(g, t, b):
        o = dot(p_q[b][:, 0:blk], vv_own[g]) + dot(p_q[b][:, blk:], vv_pair[g])
        total = o[:, HD:]
        lam = m_q[b][...] * SCALE + jnp.log2(total)
        o = (o[:, :HD] / total).astype(BF16)
        for u in range(4):
            rs_s[g, 4 * t + u, 0:64, :] = o[u * 64 : (u + 1) * 64]
            lam_v[4 * t + u, 0:1, :] = as_row(lam[u * 64 : (u + 1) * 64])

    def query_half(g):
        queries(g).wait_recv()

        @pl.when(g == 0)
        def _():
            pk_c.wait_recv()
            pv_c.wait_recv()
            fill(vv_pair, pv_v)

        q_scores(g, 0, 0)

        def step(j):
            q_scores(g, 2 * j + 1, 1)
            q_soft(0)
            q_mix(g, 2 * j, 0)
            q_scores(g, jnp.minimum(2 * j + 2, per_g - 1), 0)
            q_soft(1)
            q_mix(g, 2 * j + 1, 1)

        loop(per_g // 2, step)
        lam = lam_v[:, 0:1, :]
        hi = lam.astype(BF16).astype(F32)
        mid = (lam - hi).astype(BF16).astype(F32)
        row = iota((nch, 16, HD), 1)
        stats = jnp.where(row == 0, hi, jnp.where(row == 1, mid, jnp.where(row == 2, lam - hi - mid, 0.0)))
        rs_s[g, :, 64:80, :] = stats.astype(BF16)
        partials(g).start()
        pl.when(g == 0)(lambda: hand_on(0))
        rs_r[g, pl.ds(chip, 1)] = rs_s[g, pl.ds(chip, 1)]

    def anchors_across(g):
        anchors(g).wait_recv()
        anchor_pair(g).start()

    early = (86 - 7 * tp - 9 * (chip // 4) - 18 * (chip % 4)) // 28
    early = jnp.maximum(0, jnp.minimum(4, early))
    at_query = jnp.maximum(4, early + 1)

    pl.when(early == 0)(begin)
    lk.wait()
    lv.wait()
    fill(vv_own, v_v)
    queries_in(0).wait()
    a_scores(0, 0)

    def own_step(j):
        @pl.when((j > 0) & (j < 8))
        def _():
            queries_in(j).wait()

        @pl.when(j > 0)
        def _():
            hp = j - 1
            a_scores(hp, 1)
            a_soft(hp, 0)
            a_mix(hp, 0)
            a_scores(hp, 2)
            a_soft(hp, 1)
            a_mix(hp, 1)
            a_scores(jnp.minimum(hp + 1, 7), 0)
            a_soft(hp, 2)
            a_mix(hp, 2)

        pl.when((j == early) & (j > 0))(begin)
        @pl.when(j == at_query)
        def _():
            loop(2, query_half)
            query_kv.wait_recv()
            kv_c.start()
            w_c.start()
            lw.start()

        pl.when(j == at_query + 2)(lambda: hand_on(1))
        pl.when(j == 7)(lambda: anchors_across(0))

    loop(9, own_step)

    s_b, p_b = (sb0, sb1), (pb0, pb1)

    def b_scores(h, b):
        q = q_v[:, pl.ds(pl.multiple_of(h * HD, HD), HD)]
        s_b[b][...] = dot_t(q, an[0, h // 8].reshape(blk, HD))

    def b_soft(h, b):
        for r in range(blk // CHUNK):
            rows = slice(r * CHUNK, (r + 1) * CHUNK)
            s = s_b[b][rows, :]
            old = st_m[h, rows, :]
            m = jnp.maximum(jnp.max(s, axis=1, keepdims=True), old[:, 0:1])
            p_b[b][rows, :] = jnp.exp2((s - m) * SCALE).astype(BF16)
            st_m[h, rows, :] = jnp.exp2((old - m) * SCALE)

    def b_mix(h, b):
        o = dot(p_b[b][...], vv_anchor[h // 8])
        factor = st_m[h]
        top = factor * st_o[h, :, 0:HD] + o[:, :HD]
        total = factor * st_o[h, :, HD:] + o[:, HD:]
        out_v[:, pl.ds(pl.multiple_of(h * HD, HD), HD)] = (top / total).astype(BF16)

    def anchor_in(g):
        other = an.at[1 - core, g]
        remote(other, other, pair_s.at[4 + g], pair_r.at[4 + g], ctx=partner).wait_recv()
        vv_anchor[g, :, 0:HD] = an[1, g].reshape(blk, HD)
        vv_anchor[g, :, HD:] = jnp.ones((blk, HD), BF16)

    def self_half(g):
        count = 16 * nch
        f = iota((64, count), 1)
        side = jnp.where(f // (8 * nch) == 0, core, 1 - core)
        token = (2 * ((f // 8) % nch) + side) * 8 + f % 8
        keep = token <= 8 * me + iota((64, count), 0) % 8

        def pick(at):
            own = kvg[:, 16 * at : 16 * at + 16, :].astype(F32)
            pair = kvp[:, 16 * at : 16 * at + 16, :].astype(F32)
            both = [
                jnp.where(g == 0, a[:, 0:8, :], a[:, 8:16, :]).reshape(8 * nch, HD) for a in (own, pair)
            ]
            return jnp.concatenate(both, 0).astype(BF16)

        s = jnp.where(keep, dot_t(qg[g, chip], pick(0)), -1e30)
        m = jnp.max(s, axis=1, keepdims=True)
        p = jnp.exp2((s - m) * SCALE)
        total = jnp.sum(p, axis=1, keepdims=True)
        lam = jnp.broadcast_to(m * SCALE + jnp.log2(total), (64, HD))
        return dot(p.astype(BF16), pick(1)) / total, as_row(lam)

    def spot(share):
        hi = share.astype(BF16).astype(F32)
        return jnp.where(twice, jnp.where(first, hi, share - hi), 0.0).astype(BF16)

    def merge_half(g):
        own, own_lam = self_half(g)
        partials(g).wait_recv()
        stat = rs_r[g, :, 64:80, :].astype(F32)
        lam = stat[:, 0, :] + stat[:, 1, :] + stat[:, 2, :]
        peak = jnp.maximum(jnp.max(lam, axis=0, keepdims=True), own_lam)
        share = jnp.exp2(lam - peak)
        own_share = jnp.exp2(own_lam - peak)
        total = jnp.sum(share, axis=0, keepdims=True) + own_share
        share = share / total
        own = own.astype(BF16)
        acc = dot(spot(own_share / total), jnp.concatenate([own, own], 0))
        for j in range(0, nch, 2):
            left = jnp.concatenate([spot(share[j : j + 1]), spot(share[j + 1 : j + 2])], 1)
            a, b = rs_r[g, j, 0:64, :], rs_r[g, j + 1, 0:64, :]
            acc = acc + dot(left, jnp.concatenate([a, a, b, b], 0))
        ag[g, pl.ds(chip, 1)] = acc.astype(BF16)[None]
        merged(g).start()

    rows = 8 * nch
    part = rows // ntp

    def tp_copy(i, c):
        t = (tp + 1 + i) % ntp if c == 0 else (tp + i) % ntp
        where = {"tp": t} if c == 0 else {"tp": t, "ctx": partner}
        return remote(tp_s.at[c, t], tp_r.at[c, tp], tp_ss.at[c, i], tp_rs.at[c, tp], **where)

    def project():
        merged(0).wait_recv()
        merged(1).wait_recv()
        w_c.wait_recv()
        lw.wait()
        parts = [jnp.zeros((rows, w_v.shape[1]), F32)] * 2
        for hp in range(8):
            both = ag[hp // 4, :, 16 * (hp % 4) : 16 * (hp % 4) + 16, :].astype(F32)
            a = jnp.concatenate([both[:, 0:8, :].reshape(rows, HD), both[:, 8:16, :].reshape(rows, HD)], 1)
            for c, w in enumerate((w_v, pw_v)):
                parts[c] = parts[c] + dot(a.astype(BF16), w[hp * 2 * HD : (hp + 1) * 2 * HD, :])
        for c in range(2):
            for t in range(ntp):
                tp_s[c, t] = parts[c][t * part : (t + 1) * part].astype(BF16)
        loop(ntp - 1, lambda i: tp_copy(i, 0).start())
        loop(ntp, lambda i: tp_copy(i, 1).start())

    def anchor_step(j):
        @pl.when(j == 0)
        def _():
            kv_c.wait_recv()
            merge_half(0)

        pl.when(j == 1)(lambda: merge_half(1))
        pl.when(j == 2)(lambda: anchors_across(1))
        pl.when(j == 3)(lambda: anchor_in(1))
        pl.when(j == 4)(project)
        h = 2 * j

        @pl.when(me != 0)
        def _():
            b_scores(h + 1, 1)
            b_soft(h, 0)
            b_mix(h, 0)
            b_scores(jnp.minimum(h + 2, 15), 0)
            b_soft(h + 1, 1)
            b_mix(h + 1, 1)

        @pl.when(me == 0)
        def _():
            for k in (h, h + 1):
                value = st_o[k, :, 0:HD] / st_o[k, :, HD:]
                out_v[:, pl.ds(pl.multiple_of(k * HD, HD), HD)] = value.astype(BF16)

        result_out(j).start()

    anchor_in(0)
    b_scores(0, 0)
    loop(8, anchor_step)

    def tp_recv(c, t):
        buf = tp_r.at[c, t]
        where = {"tp": t} if c == 0 else {"tp": t, "ctx": partner}
        remote(buf, buf, tp_ss.at[c, 0], tp_rs.at[c, t], **where).wait_recv()

    loop(ntp - 1, lambda i: tp_recv(0, (tp + 1 + i) % ntp))
    loop(ntp, lambda i: tp_recv(1, i))
    tp_r[0, pl.ds(tp, 1)] = tp_s[0, pl.ds(tp, 1)]
    mine_sum = jnp.sum(tp_r[0].astype(F32), axis=0)
    pair_sum = jnp.sum(tp_r[1].astype(F32), axis=0)
    groups = part // 8
    even = jnp.where(core == 0, mine_sum, pair_sum).reshape(groups, 1, 8, -1)
    odd = jnp.where(core == 0, pair_sum, mine_sum).reshape(groups, 1, 8, -1)
    query_out[...] = jnp.concatenate([even, odd], 1).reshape(2 * part, -1).astype(BF16)

    def sent(g):
        for spread in (queries(g), anchors(g), partials(g), merged(g)):
            spread.wait_send()
        anchor_pair(g).wait_send()

        @pl.when(me == 0)
        def _():
            scatter_copies(g, 0)[1].wait_send()

            def step(i):
                ck, cv = scatter_copies(g, 1 + i)
                ck.wait_send()
                cv.wait_send()

            loop(nch - 1, step)

    loop(2, sent)
    query_kv.wait_send()
    loop(ntp - 1, lambda i: tp_copy(i, 0).wait_send())
    loop(ntp, lambda i: tp_copy(i, 1).wait_send())
    for c in (pk_c, pv_c, kv_c, w_c):
        c.wait_send()
    loop(8, lambda i: result_out(i).wait())


def an_view(ref, nch, piece):
    return ref.reshape(nch, piece, ref.shape[-1])


def body(nch, ntp, ctx_q, ctx_k, ctx_v, query_q, query_k, query_v, weight):
    blk, width = ctx_q.shape
    cols = ctx_k.shape[1]
    tq = blk // 3
    piece = blk // nch
    part = 8 * nch // ntp
    vmem = pltpu.VMEM
    dma = pltpu.SemaphoreType.DMA
    scratch = [
        vmem((blk, width), BF16), vmem((blk, cols), BF16), vmem((blk, cols), BF16), vmem(weight.shape, BF16),
        vmem((blk, cols), BF16), vmem((blk, cols), BF16), vmem(weight.shape, BF16), vmem((blk, width), BF16),
        vmem((2, blk, 2 * HD), BF16), vmem((2, blk, 2 * HD), BF16), vmem((2, blk, 2 * HD), BF16),
        vmem((2, nch, 64, HD), BF16), vmem((nch, 32, HD), BF16), vmem((nch, 32, HD), BF16),
        vmem((2, 2, nch, piece, HD), BF16),
        vmem((2, nch, 80, HD), BF16), vmem((2, nch, 80, HD), BF16), vmem((nch, 8, HD), F32),
        vmem((2, nch, 64, HD), BF16), vmem((2, ntp, part, weight.shape[1]), BF16), vmem((2, ntp, part, weight.shape[1]), BF16),
        vmem((16, blk, 2 * HD), F32), vmem((16, blk, HD), F32),
    ]
    scratch += [vmem((2 * tq, tq * i), F32) for i in (1, 2, 3)] + [vmem((2 * tq, tq * i), BF16) for i in (1, 2, 3)]
    scratch += [vmem((blk, blk), F32)] * 2 + [vmem((blk, blk), BF16)] * 2
    scratch += [vmem((256, 2 * blk), F32)] * 2 + [vmem((256, 2 * blk), BF16)] * 2 + [vmem((256, HD), F32)] * 2
    scratch += [
        dma((21,)), dma((6,)), dma((6,)), dma((9, nch)), dma((9, nch)), dma((2, 2, nch)), dma((2,)),
        dma((2, ntp)), dma((2, ntp)),
    ]
    hbm = pl.BlockSpec(memory_space=pl.ANY)
    near = pl.BlockSpec(memory_space=pltpu.VMEM)
    return pl.pallas_call(
        functools.partial(kernel, nch, ntp, blk),
        out_shape=(
            jax.ShapeDtypeStruct((blk, width), BF16),
            jax.ShapeDtypeStruct((2 * part, weight.shape[1]), BF16),
        ),
        in_specs=[hbm, hbm, hbm, near, near, near, hbm],
        out_specs=(hbm, near),
        scratch_shapes=scratch,
        compiler_params=pltpu.CompilerParams(
            collective_id=0, has_side_effects=True, vmem_limit_bytes=62 * 2**20
        ),
        name="star",
    )(
        ctx_q, ctx_k.reshape(nch, piece, cols), ctx_v.reshape(nch, piece, cols),
        query_q, query_k, query_v, weight,
    )


def solution(mesh):
    nch, ntp = mesh.shape["ctx"] // 2, mesh.shape["tp"]
    return jax.shard_map(
        functools.partial(body, nch, ntp),
        mesh=mesh,
        in_specs=(P("ctx", "tp"),) * 6 + (P("tp", "ctx"),),
        out_specs=(P("ctx", "tp"), P("tp", "ctx")),
        check_vma=False,
    )
```
